32 devices in a mesh: wide: 16 (over z, x, core), narrow: 2 (over y).
Axes of the slice: x: 2, y: 2, z: 4, core: 2. Of those that a mesh axis runs over, the one named last changes fastest.
Arguments:
- krylov: float32 [2, 16777216], P(None, ('wide', 'narrow')), may hold values from -6 to 6
- fitness_class: int32 [524288], P(('wide', 'narrow')), may hold values from 0 to 7
- rate_index: int32 [2], replicated, may hold values from 4 to 15
Outputs:
- images: float32 [2, 16777216], P(None, ('wide', 'narrow'))
The draws below stay inside these ranges and needn't reach their ends.
All inputs are finite; a program needn't handle non-finite values.
Results may differ from the reference program's by a relative error of at most 0.00014.
Values sent between devices are 32-bit elements; how exact they have to be, the bound alone decides.
A program may use at most 128 MiB of HBM per device.

```python
import jax
import jax.numpy as jnp
from jax import lax

FBLOCK = 32
ITERS = 2
GENOTYPES = 16777216


def touch_ends(result, own_key, smallest, top_value):
    index_at = [jax.random.randint(jax.random.fold_in(own_key, axis), (), 0, length) for axis, length in enumerate(result.shape)]
    longest = result.shape.index(max(result.shape))
    beside = index_at[:longest] + [(index_at[longest] + 1) % result.shape[longest]] + index_at[longest + 1:]
    return result.at[tuple(index_at)].set(smallest).at[tuple(beside)].set(top_value)


def block_scale(rng, dims, cuts, least, top_value):
    factor_of = 1.0
    for axis_at, shards_of in cuts:
        heights = jax.random.uniform(jax.random.fold_in(jax.random.fold_in(rng, 6), axis_at), (shards_of,), jnp.float32, least / len(cuts), top_value / len(cuts))
        factor_of = factor_of * jnp.repeat(jnp.exp(heights), dims[axis_at] // shards_of).reshape((-1,) + (1,) * (len(dims) - 1 - axis_at))
    return factor_of


def bell_draw(rng, dims, spread, most, split=(), kind=jnp.bfloat16):
    result = spread * jax.random.normal(rng, dims, jnp.float32)
    if split:
        result = result * block_scale(rng, dims, split, -0.22, 0.18)
    return jnp.clip(result, -most, most).astype(kind)


def setup_inputs(seed: int = 0) -> dict:
    arg_keys = jax.random.split(jax.random.key(seed), 4)
    krylov = bell_draw(arg_keys[0], (2, GENOTYPES), 1.0, 6.0, ((1, 32),), jnp.float32)
    fitness_class = touch_ends(jax.random.randint(arg_keys[1], (GENOTYPES // FBLOCK,), 0, 8), jax.random.fold_in(arg_keys[1], 1), 0, 7).astype(jnp.int32)
    rate_index = jax.random.randint(arg_keys[2], (2,), 4, 16).astype(jnp.int32)
    return {"krylov": krylov, "fitness_class": fitness_class, "rate_index": rate_index}


def mutation_rates(rate_index, total_bits):
    levels = 0.004 * (rate_index.astype(jnp.float32) + 1.0)
    position = jnp.arange(total_bits, dtype=jnp.float32)
    profile = 1.0 + 0.5 * jnp.cos(2.0 * position)
    return levels[:, None] * profile[None, :]


def kronecker(mutation, first_site, width_bits):
    middle = 1 << width_bits
    indices = jnp.arange(middle, dtype=jnp.int32)
    product = jnp.ones((mutation.shape[0], middle, middle), jnp.float32)
    for bit_pos in range(width_bits):
        column = (indices >> bit_pos) & 1
        agreeing = column[:, None] == column[None, :]
        chance = mutation[:, first_site + bit_pos][:, None, None]
        product = product * jnp.where(agreeing[None], 1.0 - chance, chance)
    return product


def split_widths(amount):
    groups = -(-amount // 7)
    common = amount // groups
    leftover = amount % groups
    return [common + 1 if number < leftover else common for number in range(groups)]


def mix_range(vectors, mutation, first_pos, amount, site_shift):
    vector_count, length = vectors.shape
    offset = first_pos
    for group_width in split_widths(amount):
        low_size = 1 << offset
        middle = 1 << group_width
        high_size = length // (low_size * middle)
        matrix = kronecker(mutation, offset + site_shift, group_width)
        if low_size == 1:
            shaped = vectors.reshape(vector_count, high_size, middle)
            mixed_out = jnp.einsum("aij,ahj->ahi", matrix, shaped, precision=lax.Precision.HIGHEST)
        else:
            shaped = vectors.reshape(vector_count, high_size, middle, low_size)
            mixed_out = jnp.einsum("aij,ahjl->ahil", matrix, shaped, precision=lax.Precision.HIGHEST)
        vectors = mixed_out.reshape(vector_count, length)
        offset = offset + group_width
    return vectors


def apply_fitness(vectors, classes):
    vector_count, length = vectors.shape
    blocks = classes.shape[0]
    scale_row = 0.5 + 0.25 * classes.astype(jnp.float32)
    shaped = vectors.reshape(vector_count, blocks, length // blocks) * scale_row[None, :, None]
    return shaped.reshape(vector_count, length)


def reference(krylov, fitness_class, rate_index):
    length = krylov.shape[1]
    total_bits = length.bit_length() - 1
    mutation = mutation_rates(rate_index, total_bits)
    vectors = krylov
    for iteration in range(ITERS):
        vectors = apply_fitness(vectors, fitness_class)
        vectors = mix_range(vectors, mutation, 0, total_bits, 0)
    return vectors
```

```python
import functools

import jax
import jax.numpy as jnp
import numpy as np
from jax import lax
from jax.experimental import pallas as pl
from jax.experimental.pallas import tpu as pltpu
from jax.sharding import PartitionSpec as P

LANES = 128
ROWS = 8
LANE_BITS = 7


def bits_of(count):
    return count.bit_length() - 1


def profile_of(total_bits):
    position = np.arange(total_bits, dtype=np.float32)
    return np.float32(1.0) + np.float32(0.5) * np.cos(np.float32(2.0) * position)


def rates_of(rate_ref, vector, profile, first, amount):
    level = 0.004 * (rate_ref[vector].astype(jnp.float32) + 1.0)
    return [level * float(profile[first + bit]) for bit in range(amount)]


def kron(rates, size):
    row = lax.broadcasted_iota(jnp.int32, (size, size), 0)
    column = lax.broadcasted_iota(jnp.int32, (size, size), 1)
    product = jnp.ones((size, size), jnp.float32)
    for bit, rate in enumerate(rates):
        agreeing = ((row >> bit) & 1) == ((column >> bit) & 1)
        product = product * jnp.where(agreeing, 1.0 - rate, rate)
    return product


def halves(values):
    high = values.astype(jnp.bfloat16)
    return high, (values - high.astype(jnp.float32)).astype(jnp.bfloat16)


def dot(left, right):
    return jnp.dot(left, right, preferred_element_type=jnp.float32)


def butterfly(values, rates):
    values = list(values)
    for bit, rate in enumerate(rates):
        step = 1 << bit
        for low in range(len(values)):
            if low & step:
                continue
            change = (values[low | step] - values[low]) * rate
            values[low] = values[low] + change
            values[low | step] = values[low | step] - change
    return values


def groups_of(bits):
    count = max(1, -(-bits // 5))
    groups, first = [], 0
    for number in range(count):
        amount = bits // count + (1 if number < bits % count else 0)
        groups.append((first, amount))
        first += amount
    return groups


def group_pass(group, bits, tiles, rates, load, store, scale=None):
    first, amount = group
    low = 1 << first
    others = (1 << bits) // (1 << amount)
    part = rates[first : first + amount]

    def body(step, carry):
        tile = step % tiles
        other = step // tiles
        base = (other // low) * (low << amount) + other % low
        index = [base + member * low for member in range(1 << amount)]
        values = butterfly([load(at, tile) for at in index], part)
        if scale is not None:
            values = [value * scale(at, tile) for value, at in zip(values, index)]
            values = butterfly(values, part)
        for at, value in zip(index, values):
            store(at, tile, value)
        return carry

    lax.fori_loop(0, others * tiles, body, 0)


def xor(left, right, bits):
    both = 0
    for bit in range(bits):
        both = both + (1 << bit) * (((left // (1 << bit)) % 2) * ((right // (1 << bit)) % 2))
    return left + right - 2 * both


def exchange_kernel(
    sizes, x_ref, class_ref, rate_ref, out_ref,
    send_a, send_b, land_a, land_b, scale_here, scale_moved, back, lane_high, lane_low,
    mid_high, mid_low, send_sem, land_sem, own_sem,
):
    wide, narrow, rows, local_bits, per_row = sizes
    count = wide * narrow
    wide_bits, narrow_bits = bits_of(wide), bits_of(narrow)
    device_bits = wide_bits + narrow_bits
    low_bits = local_bits - device_bits
    tiles = rows // ROWS
    class_rows = class_ref.shape[1]
    profile = profile_of(local_bits + device_bits)
    my_wide, my_narrow = lax.axis_index("wide"), lax.axis_index("narrow")
    me = my_wide * narrow + my_narrow

    def partner(turn):
        offset = (turn % 2) * (count // 2) + turn // 2
        to_wide = xor(my_wide, offset // narrow, wide_bits)
        to_narrow = xor(my_narrow, offset % narrow, narrow_bits)
        return offset, to_wide, to_narrow, to_wide * narrow + to_narrow

    barrier = pltpu.get_barrier_semaphore()

    def greet(turn, carry):
        _, to_wide, to_narrow, _ = partner(turn)
        pl.semaphore_signal(
            barrier, inc=1, device_id=(to_wide, to_narrow), device_id_type=pl.DeviceIdType.MESH
        )
        return carry

    lax.fori_loop(1, count, greet, 0)

    def copy(stage, turn):
        offset, to_wide, to_narrow, flat = partner(turn)
        source, target = (
            (send_a, land_a), (send_b, land_b), (back.at[0], out_ref.at[0]), (back.at[1], out_ref.at[1])
        )[stage]
        return flat, pltpu.make_async_remote_copy(
            src_ref=source.at[flat],
            dst_ref=target.at[me],
            send_sem=send_sem.at[stage, offset],
            recv_sem=land_sem.at[stage, offset],
            device_id=(to_wide, to_narrow),
            device_id_type=pl.DeviceIdType.MESH,
        )

    for vector in range(2):
        for high_ref, low_ref, first, size in (
            (lane_high, lane_low, 0, LANES),
            (mid_high, mid_low, LANE_BITS, rows),
        ):
            rates = rates_of(rate_ref, vector, profile, first, bits_of(size))
            high_ref[vector], low_ref[vector] = halves(kron(rates, size))

    def expand(compact):
        span = min(rows, LANES // per_row)
        spread = jnp.concatenate(
            [jnp.broadcast_to(compact[at : at + 1], (span, LANES)) for at in range(class_rows)], axis=0
        )
        row = lax.broadcasted_iota(jnp.int32, (rows, LANES), 0)
        column = lax.broadcasted_iota(jnp.int32, (rows, LANES), 1)
        kept = jnp.where(row % span == column // per_row, spread, 0.0).astype(jnp.bfloat16)
        source = lax.broadcasted_iota(jnp.int32, (LANES, LANES), 0)
        lane = lax.broadcasted_iota(jnp.int32, (LANES, LANES), 1)
        pick = jnp.where(source % per_row == lane // (LANES // per_row), 1.0, 0.0)
        return dot(kept, pick.astype(jnp.bfloat16))

    def spread_here(at, carry):
        compact = 0.5 + 0.25 * class_ref[at].astype(jnp.float32)
        send_a[at, rows:, :] = jnp.concatenate(
            [compact, jnp.zeros((ROWS - class_rows, LANES), jnp.float32)], axis=0
        )
        scale_here[at] = expand(compact)
        return carry

    lax.fori_loop(0, count, spread_here, 0)

    def tile_rows(tile):
        return pl.ds(pl.multiple_of(tile * ROWS, ROWS), ROWS)

    def prepare(vector, target):
        rates = rates_of(rate_ref, vector, profile, low_bits, device_bits)
        groups = groups_of(device_bits)

        def first_load(at, tile):
            start = 2 * (at * rows + tile * ROWS) + vector
            return x_ref[pl.ds(start, ROWS, stride=2), :] * scale_here[at, tile_rows(tile), :]

        def load(at, tile):
            return target[at, tile_rows(tile), :]

        def store(at, tile, value):
            target[at, tile_rows(tile), :] = value

        for number, group in enumerate(groups):
            group_pass(group, device_bits, tiles, rates, load if number else first_load, store)

    def low_mix(values, vector):
        high, low = halves(values)
        right = lane_high[vector]
        values = dot(high, right) + (dot(low, right) + dot(high, lane_low[vector]))
        high, low = halves(values)
        left = mid_high[vector]
        return dot(left, high) + (dot(left, low) + dot(mid_low[vector], high))

    def turn_over(vector, held):
        rates = rates_of(rate_ref, vector, profile, local_bits, device_bits)
        groups = groups_of(device_bits)

        def load(at, tile):
            return held[at, tile_rows(tile), :]

        def store(at, tile, value):
            held[at, tile_rows(tile), :] = value

        def scale(at, tile):
            return scale_moved[at, tile_rows(tile), :]

        for group in groups[:-1]:
            group_pass(group, device_bits, tiles, rates, load, store)
        group_pass(groups[-1], device_bits, tiles, rates, load, store, scale)
        for group in groups[:-1]:
            group_pass(group, device_bits, tiles, rates, load, store)

    prepare(0, send_a)
    pl.semaphore_wait(barrier, count - 1)

    def start_first(turn, carry):
        copy(0, turn)[1].start()
        return carry

    lax.fori_loop(1, count, start_first, 0)
    prepare(1, send_b)

    land_a[me, :rows, :] = low_mix(send_a[me, :rows, :], 0)
    scale_moved[me] = expand(send_a[me, rows : rows + class_rows, :])

    def first_arrivals(turn, carry):
        flat, arriving = copy(0, turn)
        arriving.wait_send()
        copy(1, turn)[1].start()
        arriving.wait_recv()
        land_a[flat, :rows, :] = low_mix(land_a[flat, :rows, :], 0)
        scale_moved[flat] = expand(land_a[flat, rows : rows + class_rows, :])
        return carry

    lax.fori_loop(1, count, first_arrivals, 0)
    turn_over(0, land_a)

    land_b[me] = low_mix(send_b[me], 1)
    back[0, me] = low_mix(land_a[me, :rows, :], 0)
    own_first = pltpu.make_async_copy(back.at[0, me], out_ref.at[0, me], own_sem.at[0])
    own_first.start()

    def second_arrivals(turn, carry):
        flat, arriving = copy(1, turn)
        back[0, flat] = low_mix(land_a[flat, :rows, :], 0)
        arriving.wait_send()
        copy(2, turn)[1].start()
        arriving.wait_recv()
        land_b[flat] = low_mix(land_b[flat], 1)
        return carry

    lax.fori_loop(1, count, second_arrivals, 0)
    turn_over(1, land_b)

    back[1, me] = low_mix(land_b[me], 1)
    own_second = pltpu.make_async_copy(back.at[1, me], out_ref.at[1, me], own_sem.at[1])
    own_second.start()

    def third_arrivals(turn, carry):
        flat, arriving = copy(2, turn)
        back[1, flat] = low_mix(land_b[flat], 1)
        arriving.wait_send()
        copy(3, turn)[1].start()
        return carry

    lax.fori_loop(1, count, third_arrivals, 0)
    own_first.wait()
    own_second.wait()

    def last_arrivals(turn, carry):
        copy(2, turn)[1].wait_recv()
        copy(3, turn)[1].wait()
        return carry

    lax.fori_loop(1, count, last_arrivals, 0)


def finish_kernel(sizes, profile, land_ref, rate_ref, out_ref, held):
    device_bits, low_bits = sizes
    tiles = land_ref.shape[2] // ROWS
    groups = groups_of(device_bits)

    def tile_rows(tile):
        return pl.ds(pl.multiple_of(tile * ROWS, ROWS), ROWS)

    for vector in range(2):
        rates = rates_of(rate_ref, vector, profile, low_bits, device_bits)

        def first_load(at, tile):
            return land_ref[vector, at, tile_rows(tile), :]

        def load(at, tile):
            return held[at, tile_rows(tile), :]

        def store(at, tile, value):
            held[at, tile_rows(tile), :] = value

        def last_store(at, tile, value):
            out_ref[at, pl.ds(2 * ROWS * tile + vector, ROWS, stride=2), :] = value

        for number, group in enumerate(groups):
            group_pass(
                group, device_bits, tiles, rates,
                load if number else first_load,
                last_store if number == len(groups) - 1 else store,
            )


def per_device(krylov, fitness_class, rate_index):
    vectors, length = krylov.shape
    wide, narrow = lax.axis_size("wide"), lax.axis_size("narrow")
    count = wide * narrow
    local_bits, device_bits = bits_of(length), bits_of(count)
    low_bits = local_bits - device_bits
    slab = length // count
    rows = slab // LANES
    per_row = LANES * fitness_class.shape[0] // length
    slab_classes = fitness_class.shape[0] // count
    interleaved = krylov.reshape(vectors, length // LANES, LANES).transpose(1, 0, 2)
    interleaved = interleaved.reshape(vectors * length // LANES, LANES)
    classes = fitness_class.reshape(count, slab_classes)
    if slab_classes < LANES:
        classes = jnp.pad(classes, ((0, 0), (0, LANES - slab_classes)))
    classes = classes.reshape(count, -1, LANES)
    f32, bf16 = jnp.float32, jnp.bfloat16
    vmem = pl.BlockSpec(memory_space=pltpu.VMEM)
    smem = pl.BlockSpec(memory_space=pltpu.SMEM)
    landed = pl.pallas_call(
        functools.partial(exchange_kernel, (wide, narrow, rows, local_bits, per_row)),
        out_shape=jax.ShapeDtypeStruct((vectors, count, rows, LANES), f32),
        in_specs=[vmem, vmem, smem],
        out_specs=pl.BlockSpec(memory_space=pl.ANY),
        scratch_shapes=[
            pltpu.VMEM((count, rows + ROWS, LANES), f32),
            pltpu.VMEM((count, rows, LANES), f32),
            pltpu.VMEM((count, rows + ROWS, LANES), f32),
            pltpu.VMEM((count, rows, LANES), f32),
            pltpu.VMEM((count, rows, LANES), f32),
            pltpu.VMEM((count, rows, LANES), f32),
            pltpu.VMEM((vectors, count, rows, LANES), f32),
            pltpu.VMEM((vectors, LANES, LANES), bf16),
            pltpu.VMEM((vectors, LANES, LANES), bf16),
            pltpu.VMEM((vectors, rows, rows), bf16),
            pltpu.VMEM((vectors, rows, rows), bf16),
            pltpu.SemaphoreType.DMA((4, count)),
            pltpu.SemaphoreType.DMA((4, count)),
            pltpu.SemaphoreType.DMA((2,)),
        ],
        compiler_params=pltpu.CompilerParams(
            collective_id=0, has_side_effects=True, vmem_limit_bytes=44 * 1024 * 1024
        ),
        name="exchange",
    )(interleaved, classes, rate_index)

    block = min(rows, 32)
    profile = profile_of(local_bits + device_bits)
    mixed = pl.pallas_call(
        functools.partial(finish_kernel, (device_bits, low_bits), profile),
        grid=(rows // block,),
        out_shape=jax.ShapeDtypeStruct((count, vectors * rows, LANES), f32),
        in_specs=[
            pl.BlockSpec((vectors, count, block, LANES), lambda step: (0, 0, step, 0)),
            smem,
        ],
        out_specs=pl.BlockSpec((count, vectors * block, LANES), lambda step: (0, step, 0)),
        scratch_shapes=[pltpu.VMEM((count, block, LANES), f32)],
        compiler_params=pltpu.CompilerParams(vmem_limit_bytes=40 * 1024 * 1024),
        name="finish",
    )(landed, rate_index)
    mixed = mixed.reshape(length // LANES, vectors, LANES).transpose(1, 0, 2)
    return mixed.reshape(vectors, length)


def solution(mesh):
    in_specs = (P(None, ("wide", "narrow")), P(("wide", "narrow")), P())
    out_specs = P(None, ("wide", "narrow"))
    return jax.shard_map(
        per_device, mesh=mesh, in_specs=in_specs, out_specs=out_specs, check_vma=False
    )
```

```python
import functools

import jax
import jax.numpy as jnp
import numpy as np
from jax import lax
from jax.experimental import pallas as pl
from jax.experimental.pallas import tpu as pltpu
from jax.sharding import PartitionSpec as P

LANES = 128
ROWS = 8
LANE_BITS = 7


def bits_of(count):
    return count.bit_length() - 1


def profile_of(total_bits):
    position = np.arange(total_bits, dtype=np.float32)
    return np.float32(1.0) + np.float32(0.5) * np.cos(np.float32(2.0) * position)


def rates_of(rate_ref, vector, profile, first, amount):
    level = 0.004 * (rate_ref[vector].astype(jnp.float32) + 1.0)
    return [level * float(profile[first + bit]) for bit in range(amount)]


def kron(rates, size):
    row = lax.broadcasted_iota(jnp.int32, (size, size), 0)
    column = lax.broadcasted_iota(jnp.int32, (size, size), 1)
    product = jnp.ones((size, size), jnp.float32)
    for bit, rate in enumerate(rates):
        agreeing = ((row >> bit) & 1) == ((column >> bit) & 1)
        product = product * jnp.where(agreeing, 1.0 - rate, rate)
    return product


def halves(values):
    high = values.astype(jnp.bfloat16)
    return high, (values - high.astype(jnp.float32)).astype(jnp.bfloat16)


def dot(left, right):
    return jnp.dot(left, right, preferred_element_type=jnp.float32)


def butterfly(values, rates):
    values = list(values)
    for bit, rate in enumerate(rates):
        step = 1 << bit
        for low in range(len(values)):
            if low & step:
                continue
            change = (values[low | step] - values[low]) * rate
            values[low] = values[low] + change
            values[low | step] = values[low | step] - change
    return values


def groups_of(bits):
    count = max(1, -(-bits // 5))
    groups, first = [], 0
    for number in range(count):
        amount = bits // count + (1 if number < bits % count else 0)
        groups.append((first, amount))
        first += amount
    return groups


def group_pass(group, bits, tiles, rates, load, store, scale=None):
    first, amount = group
    low = 1 << first
    others = (1 << bits) // (1 << amount)
    part = rates[first : first + amount]

    def body(step, carry):
        tile = step % tiles
        other = step // tiles
        base = (other // low) * (low << amount) + other % low
        index = [base + member * low for member in range(1 << amount)]
        values = butterfly([load(at, tile) for at in index], part)
        if scale is not None:
            values = [value * scale(at, tile) for value, at in zip(values, index)]
            values = butterfly(values, part)
        for at, value in zip(index, values):
            store(at, tile, value)
        return carry

    lax.fori_loop(0, others * tiles, body, 0)


def xor(left, right, bits):
    both = 0
    for bit in range(bits):
        both = both + (1 << bit) * (((left // (1 << bit)) % 2) * ((right // (1 << bit)) % 2))
    return left + right - 2 * both


def exchange_kernel(
    sizes, x_ref, class_ref, rate_ref, out_ref,
    send_a, send_b, land_a, land_b, scale_here, scale_moved, back, lane_high, lane_low,
    mid_high, mid_low, send_sem, land_sem, own_sem,
):
    wide, narrow, rows, local_bits, per_row = sizes
    count = wide * narrow
    wide_bits, narrow_bits = bits_of(wide), bits_of(narrow)
    device_bits = wide_bits + narrow_bits
    low_bits = local_bits - device_bits
    tiles = rows // ROWS
    class_rows = class_ref.shape[1]
    profile = profile_of(local_bits + device_bits)
    my_wide, my_narrow = lax.axis_index("wide"), lax.axis_index("narrow")
    me = my_wide * narrow + my_narrow

    swapped = my_wide % 2

    def partner(turn):
        turn = turn + swapped * (2 * (turn % 2) - 1) * (1 - turn // (count - 1))
        offset = (turn % 2) * (count // 2) + turn // 2
        to_wide = xor(my_wide, offset // narrow, wide_bits)
        to_narrow = xor(my_narrow, offset % narrow, narrow_bits)
        return offset, to_wide, to_narrow, to_wide * narrow + to_narrow

    barrier = pltpu.get_barrier_semaphore()

    def greet(turn, carry):
        _, to_wide, to_narrow, _ = partner(turn)
        pl.semaphore_signal(
            barrier, inc=1, device_id=(to_wide, to_narrow), device_id_type=pl.DeviceIdType.MESH
        )
        return carry

    lax.fori_loop(1, count, greet, 0)

    def copy(stage, turn):
        offset, to_wide, to_narrow, flat = partner(turn)
        source, target = (
            (send_a, land_a), (send_b, land_b), (back.at[0], out_ref.at[0]), (back.at[1], out_ref.at[1])
        )[stage]
        return flat, pltpu.make_async_remote_copy(
            src_ref=source.at[flat],
            dst_ref=target.at[me],
            send_sem=send_sem.at[stage, offset],
            recv_sem=land_sem.at[stage, offset],
            device_id=(to_wide, to_narrow),
            device_id_type=pl.DeviceIdType.MESH,
        )

    for vector in range(2):
        for high_ref, low_ref, first, size in (
            (lane_high, lane_low, 0, LANES),
            (mid_high, mid_low, LANE_BITS, rows),
        ):
            rates = rates_of(rate_ref, vector, profile, first, bits_of(size))
            high_ref[vector], low_ref[vector] = halves(kron(rates, size))

    def expand(compact):
        span = min(rows, LANES // per_row)
        spread = jnp.concatenate(
            [jnp.broadcast_to(compact[at : at + 1], (span, LANES)) for at in range(class_rows)], axis=0
        )
        row = lax.broadcasted_iota(jnp.int32, (rows, LANES), 0)
        column = lax.broadcasted_iota(jnp.int32, (rows, LANES), 1)
        kept = jnp.where(row % span == column // per_row, spread, 0.0).astype(jnp.bfloat16)
        source = lax.broadcasted_iota(jnp.int32, (LANES, LANES), 0)
        lane = lax.broadcasted_iota(jnp.int32, (LANES, LANES), 1)
        pick = jnp.where(source % per_row == lane // (LANES // per_row), 1.0, 0.0)
        return dot(kept, pick.astype(jnp.bfloat16))

    def spread_here(at, carry):
        compact = 0.5 + 0.25 * class_ref[at].astype(jnp.float32)
        send_a[at, rows:, :] = jnp.concatenate(
            [compact, jnp.zeros((ROWS - class_rows, LANES), jnp.float32)], axis=0
        )
        scale_here[at] = expand(compact)
        return carry

    lax.fori_loop(0, count, spread_here, 0)

    def tile_rows(tile):
        return pl.ds(pl.multiple_of(tile * ROWS, ROWS), ROWS)

    def prepare(vector, target):
        rates = rates_of(rate_ref, vector, profile, low_bits, device_bits)
        groups = groups_of(device_bits)

        def first_load(at, tile):
            start = 2 * (at * rows + tile * ROWS) + vector
            return x_ref[pl.ds(start, ROWS, stride=2), :] * scale_here[at, tile_rows(tile), :]

        def load(at, tile):
            return target[at, tile_rows(tile), :]

        def store(at, tile, value):
            target[at, tile_rows(tile), :] = value

        for number, group in enumerate(groups):
            group_pass(group, device_bits, tiles, rates, load if number else first_load, store)

    def low_mix(values, vector):
        high, low = halves(values)
        right = lane_high[vector]
        values = dot(high, right) + (dot(low, right) + dot(high, lane_low[vector]))
        high, low = halves(values)
        left = mid_high[vector]
        return dot(left, high) + (dot(left, low) + dot(mid_low[vector], high))

    def turn_over(vector, held):
        rates = rates_of(rate_ref, vector, profile, local_bits, device_bits)
        groups = groups_of(device_bits)

        def load(at, tile):
            return held[at, tile_rows(tile), :]

        def store(at, tile, value):
            held[at, tile_rows(tile), :] = value

        def scale(at, tile):
            return scale_moved[at, tile_rows(tile), :]

        for group in groups[:-1]:
            group_pass(group, device_bits, tiles, rates, load, store)
        group_pass(groups[-1], device_bits, tiles, rates, load, store, scale)
        for group in groups[:-1]:
            group_pass(group, device_bits, tiles, rates, load, store)

    prepare(0, send_a)
    pl.semaphore_wait(barrier, count - 1)

    def start_first(turn, carry):
        copy(0, turn)[1].start()
        return carry

    lax.fori_loop(1, count, start_first, 0)
    prepare(1, send_b)

    land_a[me, :rows, :] = low_mix(send_a[me, :rows, :], 0)
    scale_moved[me] = expand(send_a[me, rows : rows + class_rows, :])

    def first_arrivals(turn, carry):
        flat, arriving = copy(0, turn)
        arriving.wait_send()
        copy(1, turn)[1].start()
        arriving.wait_recv()
        land_a[flat, :rows, :] = low_mix(land_a[flat, :rows, :], 0)
        scale_moved[flat] = expand(land_a[flat, rows : rows + class_rows, :])
        return carry

    lax.fori_loop(1, count, first_arrivals, 0)
    turn_over(0, land_a)

    land_b[me] = low_mix(send_b[me], 1)
    back[0, me] = low_mix(land_a[me, :rows, :], 0)
    own_first = pltpu.make_async_copy(back.at[0, me], out_ref.at[0, me], own_sem.at[0])
    own_first.start()

    def second_arrivals(turn, carry):
        flat, arriving = copy(1, turn)
        back[0, flat] = low_mix(land_a[flat, :rows, :], 0)
        arriving.wait_send()
        copy(2, turn)[1].start()
        arriving.wait_recv()
        land_b[flat] = low_mix(land_b[flat], 1)
        return carry

    lax.fori_loop(1, count, second_arrivals, 0)
    turn_over(1, land_b)

    back[1, me] = low_mix(land_b[me], 1)
    own_second = pltpu.make_async_copy(back.at[1, me], out_ref.at[1, me], own_sem.at[1])
    own_second.start()

    def third_arrivals(turn, carry):
        flat, arriving = copy(2, turn)
        back[1, flat] = low_mix(land_b[flat], 1)
        arriving.wait_send()
        copy(3, turn)[1].start()
        return carry

    lax.fori_loop(1, count, third_arrivals, 0)
    own_first.wait()
    own_second.wait()

    def last_arrivals(turn, carry):
        copy(2, turn)[1].wait_recv()
        copy(3, turn)[1].wait()
        return carry

    lax.fori_loop(1, count, last_arrivals, 0)


def finish_kernel(sizes, profile, land_ref, rate_ref, out_ref, held):
    device_bits, low_bits = sizes
    tiles = land_ref.shape[2] // ROWS
    groups = groups_of(device_bits)

    def tile_rows(tile):
        return pl.ds(pl.multiple_of(tile * ROWS, ROWS), ROWS)

    for vector in range(2):
        rates = rates_of(rate_ref, vector, profile, low_bits, device_bits)

        def first_load(at, tile):
            return land_ref[vector, at, tile_rows(tile), :]

        def load(at, tile):
            return held[at, tile_rows(tile), :]

        def store(at, tile, value):
            held[at, tile_rows(tile), :] = value

        def last_store(at, tile, value):
            out_ref[at, pl.ds(2 * ROWS * tile + vector, ROWS, stride=2), :] = value

        for number, group in enumerate(groups):
            group_pass(
                group, device_bits, tiles, rates,
                load if number else first_load,
                last_store if number == len(groups) - 1 else store,
            )


def per_device(krylov, fitness_class, rate_index):
    vectors, length = krylov.shape
    wide, narrow = lax.axis_size("wide"), lax.axis_size("narrow")
    count = wide * narrow
    local_bits, device_bits = bits_of(length), bits_of(count)
    low_bits = local_bits - device_bits
    slab = length // count
    rows = slab // LANES
    per_row = LANES * fitness_class.shape[0] // length
    slab_classes = fitness_class.shape[0] // count
    interleaved = krylov.reshape(vectors, length // LANES, LANES).transpose(1, 0, 2)
    interleaved = interleaved.reshape(vectors * length // LANES, LANES)
    classes = fitness_class.reshape(count, slab_classes)
    if slab_classes < LANES:
        classes = jnp.pad(classes, ((0, 0), (0, LANES - slab_classes)))
    classes = classes.reshape(count, -1, LANES)
    f32, bf16 = jnp.float32, jnp.bfloat16
    vmem = pl.BlockSpec(memory_space=pltpu.VMEM)
    smem = pl.BlockSpec(memory_space=pltpu.SMEM)
    landed = pl.pallas_call(
        functools.partial(exchange_kernel, (wide, narrow, rows, local_bits, per_row)),
        out_shape=jax.ShapeDtypeStruct((vectors, count, rows, LANES), f32),
        in_specs=[vmem, vmem, smem],
        out_specs=pl.BlockSpec(memory_space=pl.ANY),
        scratch_shapes=[
            pltpu.VMEM((count, rows + ROWS, LANES), f32),
            pltpu.VMEM((count, rows, LANES), f32),
            pltpu.VMEM((count, rows + ROWS, LANES), f32),
            pltpu.VMEM((count, rows, LANES), f32),
            pltpu.VMEM((count, rows, LANES), f32),
            pltpu.VMEM((count, rows, LANES), f32),
            pltpu.VMEM((vectors, count, rows, LANES), f32),
            pltpu.VMEM((vectors, LANES, LANES), bf16),
            pltpu.VMEM((vectors, LANES, LANES), bf16),
            pltpu.VMEM((vectors, rows, rows), bf16),
            pltpu.VMEM((vectors, rows, rows), bf16),
            pltpu.SemaphoreType.DMA((4, count)),
            pltpu.SemaphoreType.DMA((4, count)),
            pltpu.SemaphoreType.DMA((2,)),
        ],
        compiler_params=pltpu.CompilerParams(
            collective_id=0, has_side_effects=True, vmem_limit_bytes=44 * 1024 * 1024
        ),
        name="exchange",
    )(interleaved, classes, rate_index)

    block = min(rows, 32)
    profile = profile_of(local_bits + device_bits)
    mixed = pl.pallas_call(
        functools.partial(finish_kernel, (device_bits, low_bits), profile),
        grid=(rows // block,),
        out_shape=jax.ShapeDtypeStruct((count, vectors * rows, LANES), f32),
        in_specs=[
            pl.BlockSpec((vectors, count, block, LANES), lambda step: (0, 0, step, 0)),
            smem,
        ],
        out_specs=pl.BlockSpec((count, vectors * block, LANES), lambda step: (0, step, 0)),
        scratch_shapes=[pltpu.VMEM((count, block, LANES), f32)],
        compiler_params=pltpu.CompilerParams(vmem_limit_bytes=40 * 1024 * 1024),
        name="finish",
    )(landed, rate_index)
    mixed = mixed.reshape(length // LANES, vectors, LANES).transpose(1, 0, 2)
    return mixed.reshape(vectors, length)


def solution(mesh):
    in_specs = (P(None, ("wide", "narrow")), P(("wide", "narrow")), P())
    out_specs = P(None, ("wide", "narrow"))
    return jax.shard_map(
        per_device, mesh=mesh, in_specs=in_specs, out_specs=out_specs, check_vma=False
    )
```

```python
import functools

import jax
import jax.numpy as jnp
import numpy as np
from jax import lax
from jax.experimental import pallas as pl
from jax.experimental.pallas import tpu as pltpu
from jax.sharding import PartitionSpec as P

LANES = 128
ROWS = 8
LANE_BITS = 7


def bits_of(count):
    return count.bit_length() - 1


def profile_of(total_bits):
    position = np.arange(total_bits, dtype=np.float32)
    return np.float32(1.0) + np.float32(0.5) * np.cos(np.float32(2.0) * position)


def rates_of(rate_ref, vector, profile, first, amount):
    level = 0.004 * (rate_ref[vector].astype(jnp.float32) + 1.0)
    return [level * float(profile[first + bit]) for bit in range(amount)]


def kron(rates, size):
    row = lax.broadcasted_iota(jnp.int32, (size, size), 0)
    column = lax.broadcasted_iota(jnp.int32, (size, size), 1)
    product = jnp.ones((size, size), jnp.float32)
    for bit, rate in enumerate(rates):
        agreeing = ((row >> bit) & 1) == ((column >> bit) & 1)
        product = product * jnp.where(agreeing, 1.0 - rate, rate)
    return product


def halves(values):
    high = values.astype(jnp.bfloat16)
    return high, (values - high.astype(jnp.float32)).astype(jnp.bfloat16)


def dot(left, right):
    return jnp.dot(left, right, preferred_element_type=jnp.float32)


def butterfly(values, rates):
    values = list(values)
    for bit, rate in enumerate(rates):
        step = 1 << bit
        for low in range(len(values)):
            if low & step:
                continue
            change = (values[low | step] - values[low]) * rate
            values[low] = values[low] + change
            values[low | step] = values[low | step] - change
    return values


def groups_of(bits):
    count = max(1, -(-bits // 5))
    groups, first = [], 0
    for number in range(count):
        amount = bits // count + (1 if number < bits % count else 0)
        groups.append((first, amount))
        first += amount
    return groups


def group_pass(group, bits, tiles, rates, load, store, scale=None, first_tile=0):
    first, amount = group
    low = 1 << first
    others = (1 << bits) // (1 << amount)
    part = rates[first : first + amount]

    def body(step, carry):
        tile = first_tile + step % tiles
        other = step // tiles
        base = (other // low) * (low << amount) + other % low
        index = [base + member * low for member in range(1 << amount)]
        values = butterfly([load(at, tile) for at in index], part)
        if scale is not None:
            values = [value * scale(at, tile) for value, at in zip(values, index)]
            values = butterfly(values, part)
        for at, value in zip(index, values):
            store(at, tile, value)
        return carry

    lax.fori_loop(0, others * tiles, body, 0)


def xor(left, right, bits):
    both = 0
    for bit in range(bits):
        both = both + (1 << bit) * (((left // (1 << bit)) % 2) * ((right // (1 << bit)) % 2))
    return left + right - 2 * both


def exchange_kernel(
    sizes, x_hbm, class_ref, rate_ref, out_ref,
    send_a, send_b, land_a, land_b, scale_here, scale_moved, back, lane_high, lane_low,
    mid_high, mid_low, held, send_sem, land_sem, own_sem, load_sem,
):
    wide, narrow, rows, local_bits, per_row = sizes
    count = wide * narrow
    wide_bits, narrow_bits = bits_of(wide), bits_of(narrow)
    device_bits = wide_bits + narrow_bits
    low_bits = local_bits - device_bits
    tiles = rows // ROWS
    class_rows = class_ref.shape[1]
    profile = profile_of(local_bits + device_bits)
    my_wide, my_narrow = lax.axis_index("wide"), lax.axis_index("narrow")
    me = my_wide * narrow + my_narrow

    def partner(turn):
        offset = (turn % 2) * (count // 2) + turn // 2
        to_wide = xor(my_wide, offset // narrow, wide_bits)
        to_narrow = xor(my_narrow, offset % narrow, narrow_bits)
        return offset, to_wide, to_narrow, to_wide * narrow + to_narrow

    chunks = min(4, tiles)
    chunk_rows = 2 * rows // chunks
    loads = []
    for chunk in range(chunks):
        part = pl.ds(chunk * chunk_rows, chunk_rows)
        loads.append(
            pltpu.make_async_copy(x_hbm.at[:, part, :], held.at[:, part, :], load_sem.at[chunk])
        )
        loads[-1].start()

    barrier = pltpu.get_barrier_semaphore()

    def greet(turn, carry):
        _, to_wide, to_narrow, _ = partner(turn)
        pl.semaphore_signal(
            barrier, inc=1, device_id=(to_wide, to_narrow), device_id_type=pl.DeviceIdType.MESH
        )
        return carry

    lax.fori_loop(1, count, greet, 0)

    def copy(stage, turn):
        offset, to_wide, to_narrow, flat = partner(turn)
        source, target = (
            (send_a, land_a), (send_b, land_b), (back.at[0], out_ref.at[0]), (back.at[1], out_ref.at[1])
        )[stage]
        return flat, pltpu.make_async_remote_copy(
            src_ref=source.at[flat],
            dst_ref=target.at[me],
            send_sem=send_sem.at[stage, offset],
            recv_sem=land_sem.at[stage, offset],
            device_id=(to_wide, to_narrow),
            device_id_type=pl.DeviceIdType.MESH,
        )

    def build_matrices():
        for vector in range(2):
            for high_ref, low_ref, first, size in (
                (lane_high, lane_low, 0, LANES),
                (mid_high, mid_low, LANE_BITS, rows),
            ):
                rates = rates_of(rate_ref, vector, profile, first, bits_of(size))
                high_ref[vector], low_ref[vector] = halves(kron(rates, size))

    def expand(compacts):
        span = min(rows, LANES // per_row)
        spread = jnp.concatenate(
            [
                jnp.broadcast_to(compact[at : at + 1], (span, LANES))
                for compact in compacts
                for at in range(class_rows)
            ],
            axis=0,
        )
        row = lax.broadcasted_iota(jnp.int32, spread.shape, 0)
        column = lax.broadcasted_iota(jnp.int32, spread.shape, 1)
        kept = jnp.where(row % span == column // per_row, spread, 0.0).astype(jnp.bfloat16)
        source = lax.broadcasted_iota(jnp.int32, (LANES, LANES), 0)
        lane = lax.broadcasted_iota(jnp.int32, (LANES, LANES), 1)
        pick = jnp.where(source % per_row == lane // (LANES // per_row), 1.0, 0.0)
        return dot(kept, pick.astype(jnp.bfloat16))

    together = min(8, count)

    def spread_here(step, carry):
        compacts = []
        for member in range(together):
            at = step * together + member
            compact = 0.5 + 0.25 * class_ref[at].astype(jnp.float32)
            send_a[at, rows:, :] = jnp.concatenate(
                [compact, jnp.zeros((ROWS - class_rows, LANES), jnp.float32)], axis=0
            )
            compacts.append(compact)
        spread = expand(compacts)
        for member in range(together):
            scale_here[step * together + member] = spread[member * rows : (member + 1) * rows]
        return carry

    lax.fori_loop(0, count // together, spread_here, 0)

    def tile_rows(tile):
        return pl.ds(pl.multiple_of(tile * ROWS, ROWS), ROWS)

    def prepare(vector, target, chunk):
        rates = rates_of(rate_ref, vector, profile, low_bits, device_bits)
        groups = groups_of(device_bits)

        def first_load(at, tile):
            pairs = pl.ds(2 * ROWS * tile + vector, ROWS, stride=2)
            return held[at, pairs, :] * scale_here[at, tile_rows(tile), :]

        def load(at, tile):
            return target[at, tile_rows(tile), :]

        def store(at, tile, value):
            target[at, tile_rows(tile), :] = value

        for number, group in enumerate(groups):
            group_pass(
                group, device_bits, tiles // chunks, rates,
                load if number else first_load, store, first_tile=chunk * (tiles // chunks),
            )

    def low_mix(slabs, vector):
        high, low = halves(jnp.concatenate(slabs, axis=0))
        right = lane_high[vector]
        values = dot(high, right) + (dot(low, right) + dot(high, lane_low[vector]))
        values = jnp.concatenate(
            [values[at * rows : (at + 1) * rows] for at in range(len(slabs))], axis=1
        )
        high, low = halves(values)
        left = mid_high[vector]
        values = dot(left, high) + (dot(left, low) + dot(mid_low[vector], high))
        return [values[:, at * LANES : (at + 1) * LANES] for at in range(len(slabs))]

    def turn_over(vector, held):
        rates = rates_of(rate_ref, vector, profile, local_bits, device_bits)
        groups = groups_of(device_bits)

        def load(at, tile):
            return held[at, tile_rows(tile), :]

        def store(at, tile, value):
            held[at, tile_rows(tile), :] = value

        def scale(at, tile):
            return scale_moved[at, tile_rows(tile), :]

        for group in groups[:-1]:
            group_pass(group, device_bits, tiles, rates, load, store)
        group_pass(groups[-1], device_bits, tiles, rates, load, store, scale)
        for group in groups[:-1]:
            group_pass(group, device_bits, tiles, rates, load, store)

    def each_pair(step):
        step(0, True)

        def body(pair, carry):
            step(pair, False)
            return carry

        lax.fori_loop(1, count // 2, body, 0)

    def turns_of(pair, with_own):
        return [2 * pair + 1] if with_own else [2 * pair, 2 * pair + 1]

    def slabs_of(pair):
        return [partner(2 * pair)[3], partner(2 * pair + 1)[3]]

    for chunk in range(chunks):
        loads[chunk].wait()
        prepare(0, send_a, chunk)
    pl.semaphore_wait(barrier, count - 1)

    def start_first(turn, carry):
        copy(0, turn)[1].start()
        return carry

    lax.fori_loop(1, count, start_first, 0)
    build_matrices()
    for chunk in range(chunks):
        prepare(1, send_b, chunk)

    def first_arrivals(pair, with_own):
        turns = turns_of(pair, with_own)
        for turn in turns:
            copy(0, turn)[1].wait_send()
            copy(1, turn)[1].start()
        for turn in turns:
            copy(0, turn)[1].wait_recv()
        slabs = slabs_of(pair)
        sources = [send_a if with_own and not at else land_a for at in range(2)]
        mixed = low_mix([source[flat, :rows, :] for source, flat in zip(sources, slabs)], 0)
        spread = expand([source[flat, rows : rows + class_rows, :] for source, flat in zip(sources, slabs)])
        for at, flat in enumerate(slabs):
            land_a[flat, :rows, :] = mixed[at]
            scale_moved[flat] = spread[at * rows : (at + 1) * rows]

    each_pair(first_arrivals)
    turn_over(0, land_a)

    own = [
        pltpu.make_async_copy(back.at[vector, me], out_ref.at[vector, me], own_sem.at[vector])
        for vector in range(2)
    ]

    def send_back(vector, landed, pair, with_own):
        slabs = slabs_of(pair)
        mixed = low_mix([landed[flat, :rows, :] for flat in slabs], vector)
        for flat, values in zip(slabs, mixed):
            back[vector, flat] = values
        if with_own:
            own[vector].start()
        for turn in turns_of(pair, with_own):
            copy(1 + vector, turn)[1].wait_send()
            copy(2 + vector, turn)[1].start()

    def second_arrivals(pair, with_own):
        send_back(0, land_a, pair, with_own)
        for turn in turns_of(pair, with_own):
            copy(1, turn)[1].wait_recv()
        slabs = slabs_of(pair)
        sources = [send_b if with_own and not at else land_b for at in range(2)]
        mixed = low_mix([source[flat] for source, flat in zip(sources, slabs)], 1)
        for flat, values in zip(slabs, mixed):
            land_b[flat] = values

    each_pair(second_arrivals)
    turn_over(1, land_b)

    def third_arrivals(pair, with_own):
        send_back(1, land_b, pair, with_own)

    each_pair(third_arrivals)
    own[0].wait()
    own[1].wait()

    def last_arrivals(turn, carry):
        copy(2, turn)[1].wait_recv()
        copy(3, turn)[1].wait()
        return carry

    lax.fori_loop(1, count, last_arrivals, 0)


def finish_kernel(sizes, profile, land_ref, rate_ref, out_ref, held):
    device_bits, low_bits = sizes
    tiles = land_ref.shape[2] // ROWS
    groups = groups_of(device_bits)

    def tile_rows(tile):
        return pl.ds(pl.multiple_of(tile * ROWS, ROWS), ROWS)

    for vector in range(2):
        rates = rates_of(rate_ref, vector, profile, low_bits, device_bits)

        def first_load(at, tile):
            return land_ref[vector, at, tile_rows(tile), :]

        def load(at, tile):
            return held[at, tile_rows(tile), :]

        def store(at, tile, value):
            held[at, tile_rows(tile), :] = value

        def last_store(at, tile, value):
            out_ref[at, pl.ds(2 * ROWS * tile + vector, ROWS, stride=2), :] = value

        for number, group in enumerate(groups):
            group_pass(
                group, device_bits, tiles, rates,
                load if number else first_load,
                last_store if number == len(groups) - 1 else store,
            )


def per_device(krylov, fitness_class, rate_index):
    vectors, length = krylov.shape
    wide, narrow = lax.axis_size("wide"), lax.axis_size("narrow")
    count = wide * narrow
    local_bits, device_bits = bits_of(length), bits_of(count)
    low_bits = local_bits - device_bits
    slab = length // count
    rows = slab // LANES
    per_row = LANES * fitness_class.shape[0] // length
    slab_classes = fitness_class.shape[0] // count
    interleaved = krylov.reshape(vectors, length // LANES, LANES).transpose(1, 0, 2)
    interleaved = interleaved.reshape(count, vectors * rows, LANES)
    classes = fitness_class.reshape(count, slab_classes)
    if slab_classes < LANES:
        classes = jnp.pad(classes, ((0, 0), (0, LANES - slab_classes)))
    classes = classes.reshape(count, -1, LANES)
    f32, bf16 = jnp.float32, jnp.bfloat16
    vmem = pl.BlockSpec(memory_space=pltpu.VMEM)
    smem = pl.BlockSpec(memory_space=pltpu.SMEM)
    landed = pl.pallas_call(
        functools.partial(exchange_kernel, (wide, narrow, rows, local_bits, per_row)),
        out_shape=jax.ShapeDtypeStruct((vectors, count, rows, LANES), f32),
        in_specs=[pl.BlockSpec(memory_space=pl.ANY), vmem, smem],
        out_specs=pl.BlockSpec(memory_space=pl.ANY),
        scratch_shapes=[
            pltpu.VMEM((count, rows + ROWS, LANES), f32),
            pltpu.VMEM((count, rows, LANES), f32),
            pltpu.VMEM((count, rows + ROWS, LANES), f32),
            pltpu.VMEM((count, rows, LANES), f32),
            pltpu.VMEM((count, rows, LANES), f32),
            pltpu.VMEM((count, rows, LANES), f32),
            pltpu.VMEM((vectors, count, rows, LANES), f32),
            pltpu.VMEM((vectors, LANES, LANES), bf16),
            pltpu.VMEM((vectors, LANES, LANES), bf16),
            pltpu.VMEM((vectors, rows, rows), bf16),
            pltpu.VMEM((vectors, rows, rows), bf16),
            pltpu.VMEM((count, vectors * rows, LANES), f32),
            pltpu.SemaphoreType.DMA((4, count)),
            pltpu.SemaphoreType.DMA((4, count)),
            pltpu.SemaphoreType.DMA((2,)),
            pltpu.SemaphoreType.DMA((4,)),
        ],
        compiler_params=pltpu.CompilerParams(
            collective_id=0, has_side_effects=True, vmem_limit_bytes=60 * 1024 * 1024
        ),
        name="exchange",
    )(interleaved, classes, rate_index)

    block = min(rows, 32)
    profile = profile_of(local_bits + device_bits)
    mixed = pl.pallas_call(
        functools.partial(finish_kernel, (device_bits, low_bits), profile),
        grid=(rows // block,),
        out_shape=jax.ShapeDtypeStruct((count, vectors * rows, LANES), f32),
        in_specs=[
            pl.BlockSpec((vectors, count, block, LANES), lambda step: (0, 0, step, 0)),
            smem,
        ],
        out_specs=pl.BlockSpec((count, vectors * block, LANES), lambda step: (0, step, 0)),
        scratch_shapes=[pltpu.VMEM((count, block, LANES), f32)],
        compiler_params=pltpu.CompilerParams(vmem_limit_bytes=60 * 1024 * 1024),
        name="finish",
    )(landed, rate_index)
    mixed = mixed.reshape(length // LANES, vectors, LANES).transpose(1, 0, 2)
    return mixed.reshape(vectors, length)


def solution(mesh):
    in_specs = (P(None, ("wide", "narrow")), P(("wide", "narrow")), P())
    out_specs = P(None, ("wide", "narrow"))
    return jax.shard_map(
        per_device, mesh=mesh, in_specs=in_specs, out_specs=out_specs, check_vma=False
    )
```

```python
import functools

import jax
import jax.numpy as jnp
import numpy as np
from jax import lax
from jax.experimental import pallas as pl
from jax.experimental.pallas import tpu as pltpu
from jax.sharding import PartitionSpec as P

LANES = 128
ROWS = 8
LANE_BITS = 7


def bits_of(count):
    return count.bit_length() - 1


def profile_of(total_bits):
    position = np.arange(total_bits, dtype=np.float32)
    return np.float32(1.0) + np.float32(0.5) * np.cos(np.float32(2.0) * position)


def rates_of(rate_ref, vector, profile, first, amount):
    level = 0.004 * (rate_ref[vector].astype(jnp.float32) + 1.0)
    return [level * float(profile[first + bit]) for bit in range(amount)]


def kron(rates, size):
    row = lax.broadcasted_iota(jnp.int32, (size, size), 0)
    column = lax.broadcasted_iota(jnp.int32, (size, size), 1)
    product = jnp.ones((size, size), jnp.float32)
    for bit, rate in enumerate(rates):
        agreeing = ((row >> bit) & 1) == ((column >> bit) & 1)
        product = product * jnp.where(agreeing, 1.0 - rate, rate)
    return product


def halves(values):
    high = values.astype(jnp.bfloat16)
    return high, (values - high.astype(jnp.float32)).astype(jnp.bfloat16)


def dot(left, right):
    return jnp.dot(left, right, preferred_element_type=jnp.float32)


def butterfly(values, rates):
    values = list(values)
    for bit, rate in enumerate(rates):
        step = 1 << bit
        for low in range(len(values)):
            if low & step:
                continue
            change = (values[low | step] - values[low]) * rate
            values[low] = values[low] + change
            values[low | step] = values[low | step] - change
    return values


def groups_of(bits):
    count = max(1, -(-bits // 5))
    groups, first = [], 0
    for number in range(count):
        amount = bits // count + (1 if number < bits % count else 0)
        groups.append((first, amount))
        first += amount
    return groups


def group_pass(group, bits, tiles, rates, load, store, scale=None, first_tile=0):
    first, amount = group
    low = 1 << first
    others = (1 << bits) // (1 << amount)
    part = rates[first : first + amount]

    def body(step, carry):
        tile = first_tile + step % tiles
        other = step // tiles
        base = (other // low) * (low << amount) + other % low
        index = [base + member * low for member in range(1 << amount)]
        values = butterfly([load(at, tile) for at in index], part)
        if scale is not None:
            values = [value * scale(at, tile) for value, at in zip(values, index)]
            values = butterfly(values, part)
        for at, value in zip(index, values):
            store(at, tile, value)
        return carry

    lax.fori_loop(0, others * tiles, body, 0)


def exchange_kernel(
    sizes, x_hbm, class_hbm, rate_ref, out_ref,
    send_a, send_b, land_a, land_b, scale_here, scale_moved, back, lane_high, lane_low,
    mid_high, mid_low, held, class_ref, send_sem, land_sem, own_sem, load_sem,
):
    wide, narrow, rows, local_bits, per_row = sizes
    count = wide * narrow
    wide_bits, narrow_bits = bits_of(wide), bits_of(narrow)
    device_bits = wide_bits + narrow_bits
    low_bits = local_bits - device_bits
    tiles = rows // ROWS
    class_rows = class_hbm.shape[1]
    profile = profile_of(local_bits + device_bits)
    my_wide, my_narrow = lax.axis_index("wide"), lax.axis_index("narrow")
    me = my_wide * narrow + my_narrow

    flips = [(1 << bit) * (1 - 2 * lax.rem(lax.div(me, 1 << bit), 2)) for bit in range(device_bits)]

    def partners(pair):
        near = me
        for bit in range(device_bits - 1):
            near = near + flips[bit] * lax.rem(lax.div(pair, 1 << bit), 2)
        return (pair, near), (pair + count // 2, near + flips[-1])

    def place(flat):
        return (lax.div(flat, narrow), lax.rem(flat, narrow))

    chunks = min(4, tiles)
    chunk_rows = 2 * rows // chunks
    class_load = pltpu.make_async_copy(class_hbm, class_ref, load_sem.at[chunks])
    class_load.start()
    loads = []
    for chunk in range(chunks):
        part = pl.ds(chunk * chunk_rows, chunk_rows)
        loads.append(
            pltpu.make_async_copy(x_hbm.at[:, part, :], held.at[:, part, :], load_sem.at[chunk])
        )
        loads[-1].start()

    barrier = pltpu.get_barrier_semaphore()

    def each_pair(step):
        step(*partners(0), True)

        def body(pair, carry):
            step(*partners(pair), False)
            return carry

        lax.fori_loop(1, count // 2, body, 0)

    def sent(near, far, own):
        return [far] if own else [far, near]

    def greet(near, far, own):
        for _, flat in sent(near, far, own):
            pl.semaphore_signal(
                barrier, inc=1, device_id=place(flat), device_id_type=pl.DeviceIdType.MESH
            )

    each_pair(greet)

    def copy(stage, turn):
        offset, flat = turn
        source, target = (
            (send_a, land_a), (send_b, land_b), (back.at[0], out_ref.at[0]), (back.at[1], out_ref.at[1])
        )[stage]
        return pltpu.make_async_remote_copy(
            src_ref=source.at[flat],
            dst_ref=target.at[me],
            send_sem=send_sem.at[stage, offset],
            recv_sem=land_sem.at[stage, offset],
            device_id=place(flat),
            device_id_type=pl.DeviceIdType.MESH,
        )

    def build_matrices():
        for vector in range(2):
            for high_ref, low_ref, first, size in (
                (lane_high, lane_low, 0, LANES),
                (mid_high, mid_low, LANE_BITS, rows),
            ):
                rates = rates_of(rate_ref, vector, profile, first, bits_of(size))
                high_ref[vector], low_ref[vector] = halves(kron(rates, size))

    def expand(compacts):
        span = min(rows, LANES // per_row)
        spread = jnp.concatenate(
            [
                jnp.broadcast_to(compact[at : at + 1], (span, LANES))
                for compact in compacts
                for at in range(class_rows)
            ],
            axis=0,
        )
        row = lax.broadcasted_iota(jnp.int32, spread.shape, 0)
        column = lax.broadcasted_iota(jnp.int32, spread.shape, 1)
        kept = jnp.where(row % span == column // per_row, spread, 0.0).astype(jnp.bfloat16)
        source = lax.broadcasted_iota(jnp.int32, (LANES, LANES), 0)
        lane = lax.broadcasted_iota(jnp.int32, (LANES, LANES), 1)
        pick = jnp.where(source % per_row == lane // (LANES // per_row), 1.0, 0.0)
        return dot(kept, pick.astype(jnp.bfloat16))

    together = min(8, count)

    def spread_here(step, carry):
        compacts = []
        for member in range(together):
            at = step * together + member
            compact = 0.5 + 0.25 * class_ref[at].astype(jnp.float32)
            send_a[at, rows:, :] = compact
            compacts.append(compact)
        spread = expand(compacts)
        for member in range(together):
            scale_here[step * together + member] = spread[member * rows : (member + 1) * rows]
        return carry

    class_load.wait()
    lax.fori_loop(0, count // together, spread_here, 0)

    def tile_rows(tile):
        return pl.ds(pl.multiple_of(tile * ROWS, ROWS), ROWS)

    def prepare(vector, target, chunk):
        rates = rates_of(rate_ref, vector, profile, low_bits, device_bits)
        groups = groups_of(device_bits)

        def first_load(at, tile):
            pairs = pl.ds(2 * ROWS * tile + vector, ROWS, stride=2)
            return held[at, pairs, :] * scale_here[at, tile_rows(tile), :]

        def load(at, tile):
            return target[at, tile_rows(tile), :]

        def store(at, tile, value):
            target[at, tile_rows(tile), :] = value

        for number, group in enumerate(groups):
            group_pass(
                group, device_bits, tiles // chunks, rates,
                load if number else first_load, store, first_tile=chunk * (tiles // chunks),
            )

    def low_mix(slabs, vector):
        high, low = halves(jnp.concatenate(slabs, axis=0))
        right = lane_high[vector]
        values = dot(high, right) + (dot(low, right) + dot(high, lane_low[vector]))
        values = jnp.concatenate(
            [values[at * rows : (at + 1) * rows] for at in range(len(slabs))], axis=1
        )
        high, low = halves(values)
        left = mid_high[vector]
        values = dot(left, high) + (dot(left, low) + dot(mid_low[vector], high))
        return [values[:, at * LANES : (at + 1) * LANES] for at in range(len(slabs))]

    def turn_over(vector, held):
        rates = rates_of(rate_ref, vector, profile, local_bits, device_bits)
        groups = groups_of(device_bits)

        def load(at, tile):
            return held[at, tile_rows(tile), :]

        def store(at, tile, value):
            held[at, tile_rows(tile), :] = value

        def scale(at, tile):
            return scale_moved[at, tile_rows(tile), :]

        for group in groups[:-1]:
            group_pass(group, device_bits, tiles, rates, load, store)
        group_pass(groups[-1], device_bits, tiles, rates, load, store, scale)
        for group in groups[:-1]:
            group_pass(group, device_bits, tiles, rates, load, store)

    for chunk in range(chunks):
        loads[chunk].wait()
        prepare(0, send_a, chunk)
    pl.semaphore_wait(barrier, count - 1)

    def start_first(near, far, own):
        for turn in sent(near, far, own):
            copy(0, turn).start()

    each_pair(start_first)
    build_matrices()
    for chunk in range(chunks):
        prepare(1, send_b, chunk)

    def first_arrivals(near, far, own):
        turns = sent(near, far, own)
        for turn in turns:
            copy(0, turn).wait_send()
            copy(1, turn).start()
        for turn in turns:
            copy(0, turn).wait_recv()
        slabs = [near[1], far[1]]
        sources = [send_a if own else land_a, land_a]
        mixed = low_mix([source[flat, :rows, :] for source, flat in zip(sources, slabs)], 0)
        spread = expand([source[flat, rows:, :] for source, flat in zip(sources, slabs)])
        for at, flat in enumerate(slabs):
            land_a[flat, :rows, :] = mixed[at]
            scale_moved[flat] = spread[at * rows : (at + 1) * rows]

    each_pair(first_arrivals)
    turn_over(0, land_a)

    kept = [
        pltpu.make_async_copy(back.at[vector, me], out_ref.at[vector, me], own_sem.at[vector])
        for vector in range(2)
    ]

    def send_back(vector, landed, near, far, own):
        slabs = [near[1], far[1]]
        mixed = low_mix([landed[flat, :rows, :] for flat in slabs], vector)
        for flat, values in zip(slabs, mixed):
            back[vector, flat] = values
        if own:
            kept[vector].start()
        for turn in sent(near, far, own):
            copy(1 + vector, turn).wait_send()
            copy(2 + vector, turn).start()

    def second_arrivals(near, far, own):
        send_back(0, land_a, near, far, own)
        for turn in sent(near, far, own):
            copy(1, turn).wait_recv()
        slabs = [near[1], far[1]]
        sources = [send_b if own else land_b, land_b]
        mixed = low_mix([source[flat] for source, flat in zip(sources, slabs)], 1)
        for flat, values in zip(slabs, mixed):
            land_b[flat] = values

    each_pair(second_arrivals)
    turn_over(1, land_b)

    def third_arrivals(near, far, own):
        send_back(1, land_b, near, far, own)

    each_pair(third_arrivals)
    kept[0].wait()
    kept[1].wait()

    def last_arrivals(near, far, own):
        for turn in sent(near, far, own):
            copy(2, turn).wait_recv()
            copy(3, turn).wait()

    each_pair(last_arrivals)


def finish_kernel(sizes, profile, land_ref, rate_ref, out_ref, held):
    device_bits, low_bits = sizes
    tiles = land_ref.shape[2] // ROWS
    groups = groups_of(device_bits)

    def tile_rows(tile):
        return pl.ds(pl.multiple_of(tile * ROWS, ROWS), ROWS)

    for vector in range(2):
        rates = rates_of(rate_ref, vector, profile, low_bits, device_bits)

        def first_load(at, tile):
            return land_ref[vector, at, tile_rows(tile), :]

        def load(at, tile):
            return held[at, tile_rows(tile), :]

        def store(at, tile, value):
            held[at, tile_rows(tile), :] = value

        def last_store(at, tile, value):
            out_ref[at, pl.ds(2 * ROWS * tile + vector, ROWS, stride=2), :] = value

        for number, group in enumerate(groups):
            group_pass(
                group, device_bits, tiles, rates,
                load if number else first_load,
                last_store if number == len(groups) - 1 else store,
            )


def per_device(krylov, fitness_class, rate_index):
    vectors, length = krylov.shape
    wide, narrow = lax.axis_size("wide"), lax.axis_size("narrow")
    count = wide * narrow
    local_bits, device_bits = bits_of(length), bits_of(count)
    low_bits = local_bits - device_bits
    slab = length // count
    rows = slab // LANES
    per_row = LANES * fitness_class.shape[0] // length
    slab_classes = fitness_class.shape[0] // count
    interleaved = krylov.reshape(vectors, length // LANES, LANES).transpose(1, 0, 2)
    interleaved = interleaved.reshape(count, vectors * rows, LANES)
    classes = fitness_class.reshape(count, slab_classes)
    if slab_classes < LANES:
        classes = jnp.pad(classes, ((0, 0), (0, LANES - slab_classes)))
    classes = classes.reshape(count, -1, LANES)
    f32, bf16 = jnp.float32, jnp.bfloat16
    smem = pl.BlockSpec(memory_space=pltpu.SMEM)
    landed = pl.pallas_call(
        functools.partial(exchange_kernel, (wide, narrow, rows, local_bits, per_row)),
        out_shape=jax.ShapeDtypeStruct((vectors, count, rows, LANES), f32),
        in_specs=[pl.BlockSpec(memory_space=pl.ANY), pl.BlockSpec(memory_space=pl.ANY), smem],
        out_specs=pl.BlockSpec(memory_space=pl.ANY),
        scratch_shapes=[
            pltpu.VMEM((count, rows + classes.shape[1], LANES), f32),
            pltpu.VMEM((count, rows, LANES), f32),
            pltpu.VMEM((count, rows + classes.shape[1], LANES), f32),
            pltpu.VMEM((count, rows, LANES), f32),
            pltpu.VMEM((count, rows, LANES), f32),
            pltpu.VMEM((count, rows, LANES), f32),
            pltpu.VMEM((vectors, count, rows, LANES), f32),
            pltpu.VMEM((vectors, LANES, LANES), bf16),
            pltpu.VMEM((vectors, LANES, LANES), bf16),
            pltpu.VMEM((vectors, rows, rows), bf16),
            pltpu.VMEM((vectors, rows, rows), bf16),
            pltpu.VMEM((count, vectors * rows, LANES), f32),
            pltpu.VMEM(classes.shape, jnp.int32),
            pltpu.SemaphoreType.DMA((4, count)),
            pltpu.SemaphoreType.DMA((4, count)),
            pltpu.SemaphoreType.DMA((2,)),
            pltpu.SemaphoreType.DMA((5,)),
        ],
        compiler_params=pltpu.CompilerParams(
            collective_id=0, has_side_effects=True, vmem_limit_bytes=60 * 1024 * 1024
        ),
        name="exchange",
    )(interleaved, classes, rate_index)

    block = min(rows, 32)
    profile = profile_of(local_bits + device_bits)
    mixed = pl.pallas_call(
        functools.partial(finish_kernel, (device_bits, low_bits), profile),
        grid=(rows // block,),
        out_shape=jax.ShapeDtypeStruct((count, vectors * rows, LANES), f32),
        in_specs=[
            pl.BlockSpec((vectors, count, block, LANES), lambda step: (0, 0, step, 0)),
            smem,
        ],
        out_specs=pl.BlockSpec((count, vectors * block, LANES), lambda step: (0, step, 0)),
        scratch_shapes=[pltpu.VMEM((count, block, LANES), f32)],
        compiler_params=pltpu.CompilerParams(vmem_limit_bytes=60 * 1024 * 1024),
        name="finish",
    )(landed, rate_index)
    mixed = mixed.reshape(length // LANES, vectors, LANES).transpose(1, 0, 2)
    return mixed.reshape(vectors, length)


def solution(mesh):
    in_specs = (P(None, ("wide", "narrow")), P(("wide", "narrow")), P())
    out_specs = P(None, ("wide", "narrow"))
    return jax.shard_map(
        per_device, mesh=mesh, in_specs=in_specs, out_specs=out_specs, check_vma=False
    )
```

```python
import functools

import jax
import jax.numpy as jnp
import numpy as np
from jax import lax
from jax.experimental import pallas as pl
from jax.experimental.pallas import tpu as pltpu
from jax.sharding import PartitionSpec as P

LANES = 128
ROWS = 8
LANE_BITS = 7


def bits_of(count):
    return count.bit_length() - 1


def profile_of(total_bits):
    position = np.arange(total_bits, dtype=np.float32)
    return np.float32(1.0) + np.float32(0.5) * np.cos(np.float32(2.0) * position)


def rates_of(rate_ref, vector, profile, first, amount):
    level = 0.004 * (rate_ref[vector].astype(jnp.float32) + 1.0)
    return [level * float(profile[first + bit]) for bit in range(amount)]


def kron(rates, size):
    row = lax.broadcasted_iota(jnp.int32, (size, size), 0)
    column = lax.broadcasted_iota(jnp.int32, (size, size), 1)
    product = jnp.ones((size, size), jnp.float32)
    for bit, rate in enumerate(rates):
        agreeing = ((row >> bit) & 1) == ((column >> bit) & 1)
        product = product * jnp.where(agreeing, 1.0 - rate, rate)
    return product


def halves(values):
    high = values.astype(jnp.bfloat16)
    return high, (values - high.astype(jnp.float32)).astype(jnp.bfloat16)


def dot(left, right):
    return jnp.dot(left, right, preferred_element_type=jnp.float32)


def butterfly(values, rates):
    values = list(values)
    for bit, rate in enumerate(rates):
        step = 1 << bit
        for low in range(len(values)):
            if low & step:
                continue
            change = (values[low | step] - values[low]) * rate
            values[low] = values[low] + change
            values[low | step] = values[low | step] - change
    return values


def groups_of(bits):
    count = max(1, -(-bits // 5))
    groups, first = [], 0
    for number in range(count):
        amount = bits // count + (1 if number < bits % count else 0)
        groups.append((first, amount))
        first += amount
    return groups


def group_pass(group, bits, tiles, rates, load, store, scale=None, first_tile=0):
    first, amount = group
    low = 1 << first
    others = (1 << bits) // (1 << amount)
    part = rates[first : first + amount]

    def body(step, carry):
        tile = first_tile + step % tiles
        other = step // tiles
        base = (other // low) * (low << amount) + other % low
        index = [base + member * low for member in range(1 << amount)]
        values = butterfly([load(at, tile) for at in index], part)
        if scale is not None:
            values = [value * scale(at, tile) for value, at in zip(values, index)]
            values = butterfly(values, part)
        for at, value in zip(index, values):
            store(at, tile, value)
        return carry

    lax.fori_loop(0, others * tiles, body, 0)


def exchange_kernel(
    sizes, x_hbm, class_hbm, rate_ref, out_ref,
    send_a, send_b, land_a, land_b, scale_here, scale_moved, back, lane_high, lane_low,
    mid_high, mid_low, held, class_ref, land_c, send_sem, land_sem, own_sem, load_sem,
):
    wide, narrow, rows, local_bits, per_row = sizes
    count = wide * narrow
    wide_bits, narrow_bits = bits_of(wide), bits_of(narrow)
    device_bits = wide_bits + narrow_bits
    low_bits = local_bits - device_bits
    tiles = rows // ROWS
    class_rows = class_hbm.shape[1]
    profile = profile_of(local_bits + device_bits)
    my_wide, my_narrow = lax.axis_index("wide"), lax.axis_index("narrow")
    me = my_wide * narrow + my_narrow

    flips = [(1 << bit) * (1 - 2 * lax.rem(lax.div(me, 1 << bit), 2)) for bit in range(device_bits)]

    def partners(pair):
        near = me
        for bit in range(device_bits - 1):
            near = near + flips[device_bits - 2 - bit] * lax.rem(lax.div(pair, 1 << bit), 2)
        return (pair, near), (pair + count // 2, near + flips[-1])

    def place(flat):
        return (lax.div(flat, narrow), lax.rem(flat, narrow))

    chunks = min(4, tiles)
    chunk_rows = 2 * rows // chunks
    class_load = pltpu.make_async_copy(class_hbm, class_ref, load_sem.at[chunks])
    class_load.start()
    loads = []
    for chunk in range(chunks):
        part = pl.ds(chunk * chunk_rows, chunk_rows)
        loads.append(
            pltpu.make_async_copy(x_hbm.at[:, part, :], held.at[:, part, :], load_sem.at[chunk])
        )
        loads[-1].start()

    barrier = pltpu.get_barrier_semaphore()

    def each_pair(step):
        step(*partners(0), True)

        def body(pair, carry):
            step(*partners(pair), False)
            return carry

        lax.fori_loop(1, count // 2, body, 0)

    def sent(near, far, own):
        return [far] if own else [far, near]

    def greet(near, far, own):
        for _, flat in sent(near, far, own):
            pl.semaphore_signal(
                barrier, inc=1, device_id=place(flat), device_id_type=pl.DeviceIdType.MESH
            )

    each_pair(greet)

    def copy(stage, turn):
        offset, flat = turn
        source, target = (
            (send_a, land_a), (send_b, land_b), (back.at[0], land_c), (back.at[1], out_ref.at[1])
        )[stage]
        return pltpu.make_async_remote_copy(
            src_ref=source.at[flat],
            dst_ref=target.at[me],
            send_sem=send_sem.at[stage, offset],
            recv_sem=land_sem.at[stage, offset],
            device_id=place(flat),
            device_id_type=pl.DeviceIdType.MESH,
        )

    def build_matrices():
        for vector in range(2):
            for high_ref, low_ref, first, size in (
                (lane_high, lane_low, 0, LANES),
                (mid_high, mid_low, LANE_BITS, rows),
            ):
                rates = rates_of(rate_ref, vector, profile, first, bits_of(size))
                high_ref[vector], low_ref[vector] = halves(kron(rates, size))

    def expand(compacts):
        span = min(rows, LANES // per_row)
        spread = jnp.concatenate(
            [
                jnp.broadcast_to(compact[at : at + 1], (span, LANES))
                for compact in compacts
                for at in range(class_rows)
            ],
            axis=0,
        )
        row = lax.broadcasted_iota(jnp.int32, spread.shape, 0)
        column = lax.broadcasted_iota(jnp.int32, spread.shape, 1)
        kept = jnp.where(row % span == column // per_row, spread, 0.0).astype(jnp.bfloat16)
        source = lax.broadcasted_iota(jnp.int32, (LANES, LANES), 0)
        lane = lax.broadcasted_iota(jnp.int32, (LANES, LANES), 1)
        pick = jnp.where(source % per_row == lane // (LANES // per_row), 1.0, 0.0)
        return dot(kept, pick.astype(jnp.bfloat16))

    together = min(8, count)

    def spread_here(step, carry):
        compacts = []
        for member in range(together):
            at = step * together + member
            compact = 0.5 + 0.25 * class_ref[at].astype(jnp.float32)
            send_a[at, rows:, :] = compact
            compacts.append(compact)
        spread = expand(compacts)
        for member in range(together):
            scale_here[step * together + member] = spread[member * rows : (member + 1) * rows]
        return carry

    class_load.wait()
    lax.fori_loop(0, count // together, spread_here, 0)

    def tile_rows(tile):
        return pl.ds(pl.multiple_of(tile * ROWS, ROWS), ROWS)

    def prepare(vector, target, chunk):
        rates = rates_of(rate_ref, vector, profile, low_bits, device_bits)
        groups = groups_of(device_bits)

        def first_load(at, tile):
            pairs = pl.ds(2 * ROWS * tile + vector, ROWS, stride=2)
            return held[at, pairs, :] * scale_here[at, tile_rows(tile), :]

        def load(at, tile):
            return target[at, tile_rows(tile), :]

        def store(at, tile, value):
            target[at, tile_rows(tile), :] = value

        for number, group in enumerate(groups):
            group_pass(
                group, device_bits, tiles // chunks, rates,
                load if number else first_load, store, first_tile=chunk * (tiles // chunks),
            )

    def low_mix(slabs, vector):
        high, low = halves(jnp.concatenate(slabs, axis=0))
        right = lane_high[vector]
        values = dot(high, right) + (dot(low, right) + dot(high, lane_low[vector]))
        values = jnp.concatenate(
            [values[at * rows : (at + 1) * rows] for at in range(len(slabs))], axis=1
        )
        high, low = halves(values)
        left = mid_high[vector]
        values = dot(left, high) + (dot(left, low) + dot(mid_low[vector], high))
        return [values[:, at * LANES : (at + 1) * LANES] for at in range(len(slabs))]

    def turn_over(vector, held):
        rates = rates_of(rate_ref, vector, profile, local_bits, device_bits)
        groups = groups_of(device_bits)

        def load(at, tile):
            return held[at, tile_rows(tile), :]

        def store(at, tile, value):
            held[at, tile_rows(tile), :] = value

        def scale(at, tile):
            return scale_moved[at, tile_rows(tile), :]

        for group in groups[:-1]:
            group_pass(group, device_bits, tiles, rates, load, store)
        group_pass(groups[-1], device_bits, tiles, rates, load, store, scale)
        for group in groups[:-1]:
            group_pass(group, device_bits, tiles, rates, load, store)

    for chunk in range(chunks):
        loads[chunk].wait()
        prepare(0, send_a, chunk)
    pl.semaphore_wait(barrier, count - 1)

    def start_first(near, far, own):
        for turn in sent(near, far, own):
            copy(0, turn).start()

    each_pair(start_first)
    build_matrices()
    for chunk in range(chunks):
        prepare(1, send_b, chunk)

    def first_arrivals(near, far, own):
        turns = sent(near, far, own)
        for turn in turns:
            copy(0, turn).wait_send()
            copy(1, turn).start()
        for turn in turns:
            copy(0, turn).wait_recv()
        slabs = [near[1], far[1]]
        sources = [send_a if own else land_a, land_a]
        mixed = low_mix([source[flat, :rows, :] for source, flat in zip(sources, slabs)], 0)
        spread = expand([source[flat, rows:, :] for source, flat in zip(sources, slabs)])
        for at, flat in enumerate(slabs):
            land_a[flat, :rows, :] = mixed[at]
            scale_moved[flat] = spread[at * rows : (at + 1) * rows]

    each_pair(first_arrivals)
    turn_over(0, land_a)

    own_copy = pltpu.make_async_copy(back.at[1, me], out_ref.at[1, me], own_sem.at[0])

    def send_back(vector, landed, near, far, own):
        slabs = [near[1], far[1]]
        mixed = low_mix([landed[flat, :rows, :] for flat in slabs], vector)
        if own and vector == 0:
            land_c[me] = mixed[0]
        else:
            back[vector, slabs[0]] = mixed[0]
        back[vector, slabs[1]] = mixed[1]
        if own and vector == 1:
            own_copy.start()
        for turn in sent(near, far, own):
            copy(1 + vector, turn).wait_send()
            copy(2 + vector, turn).start()

    def second_arrivals(near, far, own):
        send_back(0, land_a, near, far, own)
        for turn in sent(near, far, own):
            copy(1, turn).wait_recv()
        slabs = [near[1], far[1]]
        sources = [send_b if own else land_b, land_b]
        mixed = low_mix([source[flat] for source, flat in zip(sources, slabs)], 1)
        for flat, values in zip(slabs, mixed):
            land_b[flat] = values

    each_pair(second_arrivals)
    turn_over(1, land_b)

    def third_arrivals(near, far, own):
        send_back(1, land_b, near, far, own)

    each_pair(third_arrivals)
    def third_landed(near, far, own):
        for turn in sent(near, far, own):
            copy(2, turn).wait_recv()

    each_pair(third_landed)
    rates = rates_of(rate_ref, 0, profile, low_bits, device_bits)
    for group in groups_of(device_bits):
        group_pass(
            group, device_bits, tiles, rates,
            lambda at, tile: land_c[at, tile_rows(tile), :],
            lambda at, tile, value: land_c.__setitem__((at, tile_rows(tile), slice(None)), value),
        )
    first_out = pltpu.make_async_copy(land_c, out_ref.at[0], own_sem.at[1])
    first_out.start()
    own_copy.wait()

    def last_arrivals(near, far, own):
        for turn in sent(near, far, own):
            copy(3, turn).wait()

    each_pair(last_arrivals)
    first_out.wait()


def finish_kernel(sizes, profile, land_ref, rate_ref, out_ref, held):
    device_bits, low_bits = sizes
    tiles = land_ref.shape[2] // ROWS
    groups = groups_of(device_bits)

    def tile_rows(tile):
        return pl.ds(pl.multiple_of(tile * ROWS, ROWS), ROWS)

    def landed(vector):
        return lambda at, tile: land_ref[vector, at, tile_rows(tile), :]

    def final(vector):
        def store(at, tile, value):
            out_ref[at, pl.ds(2 * ROWS * tile + vector, ROWS, stride=2), :] = value

        return store

    def load(at, tile):
        return held[at, tile_rows(tile), :]

    def store(at, tile, value):
        held[at, tile_rows(tile), :] = value

    group_pass(groups[0], device_bits, tiles, [], landed(0), final(0))
    rates = rates_of(rate_ref, 1, profile, low_bits, device_bits)
    for number, group in enumerate(groups):
        group_pass(
            group, device_bits, tiles, rates,
            load if number else landed(1),
            final(1) if number == len(groups) - 1 else store,
        )


def per_device(krylov, fitness_class, rate_index):
    vectors, length = krylov.shape
    wide, narrow = lax.axis_size("wide"), lax.axis_size("narrow")
    count = wide * narrow
    local_bits, device_bits = bits_of(length), bits_of(count)
    low_bits = local_bits - device_bits
    slab = length // count
    rows = slab // LANES
    per_row = LANES * fitness_class.shape[0] // length
    slab_classes = fitness_class.shape[0] // count
    interleaved = krylov.reshape(vectors, length // LANES, LANES).transpose(1, 0, 2)
    interleaved = interleaved.reshape(count, vectors * rows, LANES)
    classes = fitness_class.reshape(count, slab_classes)
    if slab_classes < LANES:
        classes = jnp.pad(classes, ((0, 0), (0, LANES - slab_classes)))
    classes = classes.reshape(count, -1, LANES)
    f32, bf16 = jnp.float32, jnp.bfloat16
    smem = pl.BlockSpec(memory_space=pltpu.SMEM)
    landed = pl.pallas_call(
        functools.partial(exchange_kernel, (wide, narrow, rows, local_bits, per_row)),
        out_shape=jax.ShapeDtypeStruct((vectors, count, rows, LANES), f32),
        in_specs=[pl.BlockSpec(memory_space=pl.ANY), pl.BlockSpec(memory_space=pl.ANY), smem],
        out_specs=pl.BlockSpec(memory_space=pl.ANY),
        scratch_shapes=[
            pltpu.VMEM((count, rows + classes.shape[1], LANES), f32),
            pltpu.VMEM((count, rows, LANES), f32),
            pltpu.VMEM((count, rows + classes.shape[1], LANES), f32),
            pltpu.VMEM((count, rows, LANES), f32),
            pltpu.VMEM((count, rows, LANES), f32),
            pltpu.VMEM((count, rows, LANES), f32),
            pltpu.VMEM((vectors, count, rows, LANES), f32),
            pltpu.VMEM((vectors, LANES, LANES), bf16),
            pltpu.VMEM((vectors, LANES, LANES), bf16),
            pltpu.VMEM((vectors, rows, rows), bf16),
            pltpu.VMEM((vectors, rows, rows), bf16),
            pltpu.VMEM((count, vectors * rows, LANES), f32),
            pltpu.VMEM(classes.shape, jnp.int32),
            pltpu.VMEM((count, rows, LANES), f32),
            pltpu.SemaphoreType.DMA((4, count)),
            pltpu.SemaphoreType.DMA((4, count)),
            pltpu.SemaphoreType.DMA((2,)),
            pltpu.SemaphoreType.DMA((5,)),
        ],
        compiler_params=pltpu.CompilerParams(
            collective_id=0, has_side_effects=True, vmem_limit_bytes=60 * 1024 * 1024
        ),
        name="exchange",
    )(interleaved, classes, rate_index)

    block = min(rows, 32)
    profile = profile_of(local_bits + device_bits)
    mixed = pl.pallas_call(
        functools.partial(finish_kernel, (device_bits, low_bits), profile),
        grid=(rows // block,),
        out_shape=jax.ShapeDtypeStruct((count, vectors * rows, LANES), f32),
        in_specs=[
            pl.BlockSpec((vectors, count, block, LANES), lambda step: (0, 0, step, 0)),
            smem,
        ],
        out_specs=pl.BlockSpec((count, vectors * block, LANES), lambda step: (0, step, 0)),
        scratch_shapes=[pltpu.VMEM((count, block, LANES), f32)],
        compiler_params=pltpu.CompilerParams(vmem_limit_bytes=60 * 1024 * 1024),
        name="finish",
    )(landed, rate_index)
    mixed = mixed.reshape(length // LANES, vectors, LANES).transpose(1, 0, 2)
    return mixed.reshape(vectors, length)


def solution(mesh):
    in_specs = (P(None, ("wide", "narrow")), P(("wide", "narrow")), P())
    out_specs = P(None, ("wide", "narrow"))
    return jax.shard_map(
        per_device, mesh=mesh, in_specs=in_specs, out_specs=out_specs, check_vma=False
    )
```

```python
import functools

import jax
import jax.numpy as jnp
import numpy as np
from jax import lax
from jax.experimental import pallas as pl
from jax.experimental.pallas import tpu as pltpu
from jax.sharding import PartitionSpec as P

LANES = 128
ROWS = 8
LANE_BITS = 7


def bits_of(count):
    return count.bit_length() - 1


def profile_of(total_bits):
    position = np.arange(total_bits, dtype=np.float32)
    return np.float32(1.0) + np.float32(0.5) * np.cos(np.float32(2.0) * position)


def rates_of(rate_ref, vector, profile, first, amount):
    level = 0.004 * (rate_ref[vector].astype(jnp.float32) + 1.0)
    return [level * float(profile[first + bit]) for bit in range(amount)]


def kron(rates, size):
    row = lax.broadcasted_iota(jnp.int32, (size, size), 0)
    column = lax.broadcasted_iota(jnp.int32, (size, size), 1)
    product = jnp.ones((size, size), jnp.float32)
    for bit, rate in enumerate(rates):
        agreeing = ((row >> bit) & 1) == ((column >> bit) & 1)
        product = product * jnp.where(agreeing, 1.0 - rate, rate)
    return product


def halves(values):
    high = values.astype(jnp.bfloat16)
    return high, (values - high.astype(jnp.float32)).astype(jnp.bfloat16)


def dot(left, right):
    return jnp.dot(left, right, preferred_element_type=jnp.float32)


def butterfly(values, rates):
    values = list(values)
    for bit, rate in enumerate(rates):
        step = 1 << bit
        for low in range(len(values)):
            if low & step:
                continue
            change = (values[low | step] - values[low]) * rate
            values[low] = values[low] + change
            values[low | step] = values[low | step] - change
    return values


def groups_of(bits):
    count = max(1, -(-bits // 5))
    groups, first = [], 0
    for number in range(count):
        amount = bits // count + (1 if number < bits % count else 0)
        groups.append((first, amount))
        first += amount
    return groups


def group_pass(group, bits, tiles, rates, load, store, scale=None, first_tile=0):
    first, amount = group
    low = 1 << first
    others = (1 << bits) // (1 << amount)
    part = rates[first : first + amount]

    def body(step, carry):
        tile = first_tile + step % tiles
        other = step // tiles
        base = (other // low) * (low << amount) + other % low
        index = [base + member * low for member in range(1 << amount)]
        values = butterfly([load(at, tile) for at in index], part)
        if scale is not None:
            values = [value * scale(at, tile) for value, at in zip(values, index)]
            values = butterfly(values, part)
        for at, value in zip(index, values):
            store(at, tile, value)
        return carry

    lax.fori_loop(0, others * tiles, body, 0)


def exchange_kernel(
    sizes, x_hbm, class_hbm, rate_ref, out_ref,
    send_a, send_b, land_a, land_b, scale_here, scale_moved, back, lane_high, lane_low,
    mid_high, mid_low, held, class_ref, land_c, send_sem, land_sem, own_sem, load_sem,
):
    wide, narrow, rows, local_bits, per_row = sizes
    count = wide * narrow
    wide_bits, narrow_bits = bits_of(wide), bits_of(narrow)
    device_bits = wide_bits + narrow_bits
    low_bits = local_bits - device_bits
    tiles = rows // ROWS
    class_rows = class_hbm.shape[1]
    profile = profile_of(local_bits + device_bits)
    my_wide, my_narrow = lax.axis_index("wide"), lax.axis_index("narrow")
    me = my_wide * narrow + my_narrow

    flips = [(1 << bit) * (1 - 2 * lax.rem(lax.div(me, 1 << bit), 2)) for bit in range(device_bits)]

    def partners(pair, far):
        first = me + flips[-1] if far else me
        for bit in range(1, device_bits - 1):
            first = first + flips[bit] * lax.rem(lax.div(pair, 1 << (bit - 1)), 2)
        offset = 2 * pair + (count // 2 if far else 0)
        return (offset, first), (offset + 1, first + flips[0])

    def place(flat):
        return (lax.div(flat, narrow), lax.rem(flat, narrow))

    chunks = min(4, tiles)
    chunk_rows = 2 * rows // chunks
    class_load = pltpu.make_async_copy(class_hbm, class_ref, load_sem.at[chunks])
    class_load.start()
    loads = []
    for chunk in range(chunks):
        part = pl.ds(chunk * chunk_rows, chunk_rows)
        loads.append(
            pltpu.make_async_copy(x_hbm.at[:, part, :], held.at[:, part, :], load_sem.at[chunk])
        )
        loads[-1].start()

    barrier = pltpu.get_barrier_semaphore()

    def each_pair(step):
        def far_body(pair, carry):
            step(*partners(pair, True), False)
            return carry

        def near_body(pair, carry):
            step(*partners(pair, False), False)
            return carry

        lax.fori_loop(0, count // 4, far_body, 0)
        step(*partners(0, False), True)
        lax.fori_loop(1, count // 4, near_body, 0)

    def sent(first, second, own):
        return [second] if own else [first, second]

    def greet(first, second, own):
        for _, flat in sent(first, second, own):
            pl.semaphore_signal(
                barrier, inc=1, device_id=place(flat), device_id_type=pl.DeviceIdType.MESH
            )

    each_pair(greet)

    def copy(stage, turn):
        offset, flat = turn
        source, target = (
            (send_a, land_a), (send_b, land_b), (back.at[0], land_c), (back.at[1], out_ref.at[1])
        )[stage]
        return pltpu.make_async_remote_copy(
            src_ref=source.at[flat],
            dst_ref=target.at[me],
            send_sem=send_sem.at[stage, offset],
            recv_sem=land_sem.at[stage, offset],
            device_id=place(flat),
            device_id_type=pl.DeviceIdType.MESH,
        )

    def build_matrices():
        for vector in range(2):
            for high_ref, low_ref, first, size in (
                (lane_high, lane_low, 0, LANES),
                (mid_high, mid_low, LANE_BITS, rows),
            ):
                rates = rates_of(rate_ref, vector, profile, first, bits_of(size))
                high_ref[vector], low_ref[vector] = halves(kron(rates, size))

    def expand(compacts):
        span = min(rows, LANES // per_row)
        spread = jnp.concatenate(
            [
                jnp.broadcast_to(compact[at : at + 1], (span, LANES))
                for compact in compacts
                for at in range(class_rows)
            ],
            axis=0,
        )
        row = lax.broadcasted_iota(jnp.int32, spread.shape, 0)
        column = lax.broadcasted_iota(jnp.int32, spread.shape, 1)
        kept = jnp.where(row % span == column // per_row, spread, 0.0).astype(jnp.bfloat16)
        source = lax.broadcasted_iota(jnp.int32, (LANES, LANES), 0)
        lane = lax.broadcasted_iota(jnp.int32, (LANES, LANES), 1)
        pick = jnp.where(source % per_row == lane // (LANES // per_row), 1.0, 0.0)
        return dot(kept, pick.astype(jnp.bfloat16))

    together = min(8, count)

    def spread_here(step, carry):
        compacts = []
        for member in range(together):
            at = step * together + member
            compact = 0.5 + 0.25 * class_ref[at].astype(jnp.float32)
            send_a[at, rows:, :] = compact
            compacts.append(compact)
        spread = expand(compacts)
        for member in range(together):
            scale_here[step * together + member] = spread[member * rows : (member + 1) * rows]
        return carry

    class_load.wait()
    lax.fori_loop(0, count // together, spread_here, 0)

    def tile_rows(tile):
        return pl.ds(pl.multiple_of(tile * ROWS, ROWS), ROWS)

    def prepare(vector, target, chunk):
        rates = rates_of(rate_ref, vector, profile, low_bits, device_bits)
        groups = groups_of(device_bits)

        def first_load(at, tile):
            pairs = pl.ds(2 * ROWS * tile + vector, ROWS, stride=2)
            return held[at, pairs, :] * scale_here[at, tile_rows(tile), :]

        def load(at, tile):
            return target[at, tile_rows(tile), :]

        def store(at, tile, value):
            target[at, tile_rows(tile), :] = value

        for number, group in enumerate(groups):
            group_pass(
                group, device_bits, tiles // chunks, rates,
                load if number else first_load, store, first_tile=chunk * (tiles // chunks),
            )

    def low_mix(slabs, vector):
        high, low = halves(jnp.concatenate(slabs, axis=0))
        right = lane_high[vector]
        values = dot(high, right) + (dot(low, right) + dot(high, lane_low[vector]))
        values = jnp.concatenate(
            [values[at * rows : (at + 1) * rows] for at in range(len(slabs))], axis=1
        )
        high, low = halves(values)
        left = mid_high[vector]
        values = dot(left, high) + (dot(left, low) + dot(mid_low[vector], high))
        return [values[:, at * LANES : (at + 1) * LANES] for at in range(len(slabs))]

    def turn_over(vector, held):
        rates = rates_of(rate_ref, vector, profile, local_bits, device_bits)
        groups = groups_of(device_bits)

        def load(at, tile):
            return held[at, tile_rows(tile), :]

        def store(at, tile, value):
            held[at, tile_rows(tile), :] = value

        def scale(at, tile):
            return scale_moved[at, tile_rows(tile), :]

        for group in groups[:-1]:
            group_pass(group, device_bits, tiles, rates, load, store)
        group_pass(groups[-1], device_bits, tiles, rates, load, store, scale)
        for group in groups[:-1]:
            group_pass(group, device_bits, tiles, rates, load, store)

    for chunk in range(chunks):
        loads[chunk].wait()
        prepare(0, send_a, chunk)
    pl.semaphore_wait(barrier, count - 1)

    def start_first(first, second, own):
        for turn in sent(first, second, own):
            copy(0, turn).start()

    each_pair(start_first)
    build_matrices()
    for chunk in range(chunks):
        prepare(1, send_b, chunk)

    def first_arrivals(first, second, own):
        turns = sent(first, second, own)
        for turn in turns:
            copy(0, turn).wait_send()
            copy(1, turn).start()
        for turn in turns:
            copy(0, turn).wait_recv()
        slabs = [first[1], second[1]]
        sources = [send_a if own else land_a, land_a]
        mixed = low_mix([source[flat, :rows, :] for source, flat in zip(sources, slabs)], 0)
        spread = expand([source[flat, rows:, :] for source, flat in zip(sources, slabs)])
        for at, flat in enumerate(slabs):
            land_a[flat, :rows, :] = mixed[at]
            scale_moved[flat] = spread[at * rows : (at + 1) * rows]

    each_pair(first_arrivals)
    turn_over(0, land_a)

    own_copy = pltpu.make_async_copy(back.at[1, me], out_ref.at[1, me], own_sem.at[0])

    def send_back(vector, landed, first, second, own):
        slabs = [first[1], second[1]]
        mixed = low_mix([landed[flat, :rows, :] for flat in slabs], vector)
        if own and vector == 0:
            land_c[me] = mixed[0]
        else:
            back[vector, slabs[0]] = mixed[0]
        back[vector, slabs[1]] = mixed[1]
        if own and vector == 1:
            own_copy.start()
        for turn in sent(first, second, own):
            copy(1 + vector, turn).wait_send()
            copy(2 + vector, turn).start()

    def second_arrivals(first, second, own):
        send_back(0, land_a, first, second, own)
        for turn in sent(first, second, own):
            copy(1, turn).wait_recv()
        slabs = [first[1], second[1]]
        sources = [send_b if own else land_b, land_b]
        mixed = low_mix([source[flat] for source, flat in zip(sources, slabs)], 1)
        for flat, values in zip(slabs, mixed):
            land_b[flat] = values

    each_pair(second_arrivals)
    turn_over(1, land_b)

    def third_arrivals(first, second, own):
        send_back(1, land_b, first, second, own)

    each_pair(third_arrivals)
    def third_landed(first, second, own):
        for turn in sent(first, second, own):
            copy(2, turn).wait_recv()

    each_pair(third_landed)
    rates = rates_of(rate_ref, 0, profile, low_bits, device_bits)
    for group in groups_of(device_bits):
        group_pass(
            group, device_bits, tiles, rates,
            lambda at, tile: land_c[at, tile_rows(tile), :],
            lambda at, tile, value: land_c.__setitem__((at, tile_rows(tile), slice(None)), value),
        )
    first_out = pltpu.make_async_copy(land_c, out_ref.at[0], own_sem.at[1])
    first_out.start()
    own_copy.wait()

    def last_arrivals(first, second, own):
        for turn in sent(first, second, own):
            copy(3, turn).wait()

    each_pair(last_arrivals)
    first_out.wait()


def finish_kernel(sizes, profile, land_ref, rate_ref, out_ref, held):
    device_bits, low_bits = sizes
    tiles = land_ref.shape[2] // ROWS
    groups = groups_of(device_bits)

    def tile_rows(tile):
        return pl.ds(pl.multiple_of(tile * ROWS, ROWS), ROWS)

    def landed(vector):
        return lambda at, tile: land_ref[vector, at, tile_rows(tile), :]

    def final(vector):
        def store(at, tile, value):
            out_ref[at, pl.ds(2 * ROWS * tile + vector, ROWS, stride=2), :] = value

        return store

    def load(at, tile):
        return held[at, tile_rows(tile), :]

    def store(at, tile, value):
        held[at, tile_rows(tile), :] = value

    group_pass(groups[0], device_bits, tiles, [], landed(0), final(0))
    rates = rates_of(rate_ref, 1, profile, low_bits, device_bits)
    for number, group in enumerate(groups):
        group_pass(
            group, device_bits, tiles, rates,
            load if number else landed(1),
            final(1) if number == len(groups) - 1 else store,
        )


def per_device(krylov, fitness_class, rate_index):
    vectors, length = krylov.shape
    wide, narrow = lax.axis_size("wide"), lax.axis_size("narrow")
    count = wide * narrow
    local_bits, device_bits = bits_of(length), bits_of(count)
    low_bits = local_bits - device_bits
    slab = length // count
    rows = slab // LANES
    per_row = LANES * fitness_class.shape[0] // length
    slab_classes = fitness_class.shape[0] // count
    interleaved = krylov.reshape(vectors, length // LANES, LANES).transpose(1, 0, 2)
    interleaved = interleaved.reshape(count, vectors * rows, LANES)
    classes = fitness_class.reshape(count, slab_classes)
    if slab_classes < LANES:
        classes = jnp.pad(classes, ((0, 0), (0, LANES - slab_classes)))
    classes = classes.reshape(count, -1, LANES)
    f32, bf16 = jnp.float32, jnp.bfloat16
    smem = pl.BlockSpec(memory_space=pltpu.SMEM)
    landed = pl.pallas_call(
        functools.partial(exchange_kernel, (wide, narrow, rows, local_bits, per_row)),
        out_shape=jax.ShapeDtypeStruct((vectors, count, rows, LANES), f32),
        in_specs=[pl.BlockSpec(memory_space=pl.ANY), pl.BlockSpec(memory_space=pl.ANY), smem],
        out_specs=pl.BlockSpec(memory_space=pl.ANY),
        scratch_shapes=[
            pltpu.VMEM((count, rows + classes.shape[1], LANES), f32),
            pltpu.VMEM((count, rows, LANES), f32),
            pltpu.VMEM((count, rows + classes.shape[1], LANES), f32),
            pltpu.VMEM((count, rows, LANES), f32),
            pltpu.VMEM((count, rows, LANES), f32),
            pltpu.VMEM((count, rows, LANES), f32),
            pltpu.VMEM((vectors, count, rows, LANES), f32),
            pltpu.VMEM((vectors, LANES, LANES), bf16),
            pltpu.VMEM((vectors, LANES, LANES), bf16),
            pltpu.VMEM((vectors, rows, rows), bf16),
            pltpu.VMEM((vectors, rows, rows), bf16),
            pltpu.VMEM((count, vectors * rows, LANES), f32),
            pltpu.VMEM(classes.shape, jnp.int32),
            pltpu.VMEM((count, rows, LANES), f32),
            pltpu.SemaphoreType.DMA((4, count)),
            pltpu.SemaphoreType.DMA((4, count)),
            pltpu.SemaphoreType.DMA((2,)),
            pltpu.SemaphoreType.DMA((5,)),
        ],
        compiler_params=pltpu.CompilerParams(
            collective_id=0, has_side_effects=True, vmem_limit_bytes=60 * 1024 * 1024
        ),
        name="exchange",
    )(interleaved, classes, rate_index)

    block = min(rows, 16)
    profile = profile_of(local_bits + device_bits)
    mixed = pl.pallas_call(
        functools.partial(finish_kernel, (device_bits, low_bits), profile),
        grid=(rows // block,),
        out_shape=jax.ShapeDtypeStruct((count, vectors * rows, LANES), f32),
        in_specs=[
            pl.BlockSpec((vectors, count, block, LANES), lambda step: (0, 0, step, 0)),
            smem,
        ],
        out_specs=pl.BlockSpec((count, vectors * block, LANES), lambda step: (0, step, 0)),
        scratch_shapes=[pltpu.VMEM((count, block, LANES), f32)],
        compiler_params=pltpu.CompilerParams(vmem_limit_bytes=60 * 1024 * 1024),
        name="finish",
    )(landed, rate_index)
    mixed = mixed.reshape(length // LANES, vectors, LANES).transpose(1, 0, 2)
    return mixed.reshape(vectors, length)


def solution(mesh):
    in_specs = (P(None, ("wide", "narrow")), P(("wide", "narrow")), P())
    out_specs = P(None, ("wide", "narrow"))
    return jax.shard_map(
        per_device, mesh=mesh, in_specs=in_specs, out_specs=out_specs, check_vma=False
    )
```

```python
import functools

import jax
import jax.numpy as jnp
import numpy as np
from jax import lax
from jax.experimental import pallas as pl
from jax.experimental.pallas import tpu as pltpu
from jax.sharding import PartitionSpec as P

LANES = 128
ROWS = 8
LANE_BITS = 7


def bits_of(count):
    return count.bit_length() - 1


def profile_of(total_bits):
    position = np.arange(total_bits, dtype=np.float32)
    return np.float32(1.0) + np.float32(0.5) * np.cos(np.float32(2.0) * position)


def rates_of(rate_ref, vector, profile, first, amount):
    level = 0.004 * (rate_ref[vector].astype(jnp.float32) + 1.0)
    return [level * float(profile[first + bit]) for bit in range(amount)]


def kron(rates, size):
    row = lax.broadcasted_iota(jnp.int32, (size, size), 0)
    column = lax.broadcasted_iota(jnp.int32, (size, size), 1)
    product = jnp.ones((size, size), jnp.float32)
    for bit, rate in enumerate(rates):
        agreeing = ((row >> bit) & 1) == ((column >> bit) & 1)
        product = product * jnp.where(agreeing, 1.0 - rate, rate)
    return product


def halves(values):
    high = values.astype(jnp.bfloat16)
    return high, (values - high.astype(jnp.float32)).astype(jnp.bfloat16)


def dot(left, right):
    return jnp.dot(left, right, preferred_element_type=jnp.float32)


def butterfly(values, rates):
    values = list(values)
    for bit, rate in enumerate(rates):
        step = 1 << bit
        for low in range(len(values)):
            if low & step:
                continue
            change = (values[low | step] - values[low]) * rate
            values[low] = values[low] + change
            values[low | step] = values[low | step] - change
    return values


def groups_of(bits):
    count = max(1, -(-bits // 5))
    groups, first = [], 0
    for number in range(count):
        amount = bits // count + (1 if number < bits % count else 0)
        groups.append((first, amount))
        first += amount
    return groups


def group_pass(group, bits, tiles, rates, load, store, scale=None, first_tile=0):
    first, amount = group
    low = 1 << first
    others = (1 << bits) // (1 << amount)
    part = rates[first : first + amount]

    def body(step, carry):
        tile = first_tile + step % tiles
        other = step // tiles
        base = (other // low) * (low << amount) + other % low
        index = [base + member * low for member in range(1 << amount)]
        values = butterfly([load(at, tile) for at in index], part)
        if scale is not None:
            values = [value * scale(at, tile) for value, at in zip(values, index)]
            values = butterfly(values, part)
        for at, value in zip(index, values):
            store(at, tile, value)
        return carry

    lax.fori_loop(0, others * tiles, body, 0)


def exchange_kernel(
    sizes, x_hbm, class_hbm, rate_ref, out_ref,
    send_a, send_b, land_a, land_b, scale_here, scale_moved, back, lane_high, lane_low,
    mid_high, mid_low, held, class_ref, land_c, send_sem, land_sem, own_sem, load_sem,
):
    wide, narrow, rows, local_bits, per_row = sizes
    count = wide * narrow
    wide_bits, narrow_bits = bits_of(wide), bits_of(narrow)
    device_bits = wide_bits + narrow_bits
    low_bits = local_bits - device_bits
    tiles = rows // ROWS
    class_rows = class_hbm.shape[1]
    profile = profile_of(local_bits + device_bits)
    my_wide, my_narrow = lax.axis_index("wide"), lax.axis_index("narrow")
    me = my_wide * narrow + my_narrow

    flips = [(1 << bit) * (1 - 2 * lax.rem(lax.div(me, 1 << bit), 2)) for bit in range(device_bits)]

    def partners(pair):
        near = me
        for bit in range(device_bits - 1):
            near = near + flips[bit] * lax.rem(lax.div(pair, 1 << bit), 2)
        return (pair, near), (pair + count // 2, near + flips[-1])

    def place(flat):
        return (lax.div(flat, narrow), lax.rem(flat, narrow))

    chunks = min(4, tiles)
    chunk_rows = 2 * rows // chunks
    class_load = pltpu.make_async_copy(class_hbm, class_ref, load_sem.at[chunks])
    class_load.start()
    loads = []
    for chunk in range(chunks):
        part = pl.ds(chunk * chunk_rows, chunk_rows)
        loads.append(
            pltpu.make_async_copy(x_hbm.at[:, part, :], held.at[:, part, :], load_sem.at[chunk])
        )
        loads[-1].start()

    barrier = pltpu.get_barrier_semaphore()

    def each_pair(step):
        step(*partners(0), True)

        def body(pair, carry):
            step(*partners(pair), False)
            return carry

        lax.fori_loop(1, count // 2, body, 0)

    def sent(near, far, own):
        return [far] if own else [far, near]

    def greet(near, far, own):
        for _, flat in sent(near, far, own):
            pl.semaphore_signal(
                barrier, inc=1, device_id=place(flat), device_id_type=pl.DeviceIdType.MESH
            )

    each_pair(greet)

    def copy(stage, turn):
        offset, flat = turn
        source, target = (
            (send_a, land_a), (send_b, land_b), (back.at[0], land_c), (back.at[1], out_ref.at[1])
        )[stage]
        return pltpu.make_async_remote_copy(
            src_ref=source.at[flat],
            dst_ref=target.at[me],
            send_sem=send_sem.at[stage, offset],
            recv_sem=land_sem.at[stage, offset],
            device_id=place(flat),
            device_id_type=pl.DeviceIdType.MESH,
        )

    def build_matrices():
        for vector in range(2):
            for high_ref, low_ref, first, size in (
                (lane_high, lane_low, 0, LANES),
                (mid_high, mid_low, LANE_BITS, rows),
            ):
                rates = rates_of(rate_ref, vector, profile, first, bits_of(size))
                high_ref[vector], low_ref[vector] = halves(kron(rates, size))

    def expand(compacts):
        span = min(rows, LANES // per_row)
        spread = jnp.concatenate(
            [
                jnp.broadcast_to(compact[at : at + 1], (span, LANES))
                for compact in compacts
                for at in range(class_rows)
            ],
            axis=0,
        )
        row = lax.broadcasted_iota(jnp.int32, spread.shape, 0)
        column = lax.broadcasted_iota(jnp.int32, spread.shape, 1)
        kept = jnp.where(row % span == column // per_row, spread, 0.0).astype(jnp.bfloat16)
        source = lax.broadcasted_iota(jnp.int32, (LANES, LANES), 0)
        lane = lax.broadcasted_iota(jnp.int32, (LANES, LANES), 1)
        pick = jnp.where(source % per_row == lane // (LANES // per_row), 1.0, 0.0)
        return dot(kept, pick.astype(jnp.bfloat16))

    together = min(8, count)

    def spread_here(step, carry):
        compacts = []
        for member in range(together):
            at = step * together + member
            compact = 0.5 + 0.25 * class_ref[at].astype(jnp.float32)
            send_a[at, rows:, :] = compact
            compacts.append(compact)
        spread = expand(compacts)
        for member in range(together):
            scale_here[step * together + member] = spread[member * rows : (member + 1) * rows]
        return carry

    class_load.wait()
    lax.fori_loop(0, count // together, spread_here, 0)

    def tile_rows(tile):
        return pl.ds(pl.multiple_of(tile * ROWS, ROWS), ROWS)

    def prepare(vector, target, chunk):
        rates = rates_of(rate_ref, vector, profile, low_bits, device_bits)
        groups = groups_of(device_bits)

        def first_load(at, tile):
            pairs = pl.ds(2 * ROWS * tile + vector, ROWS, stride=2)
            return held[at, pairs, :] * scale_here[at, tile_rows(tile), :]

        def load(at, tile):
            return target[at, tile_rows(tile), :]

        def store(at, tile, value):
            target[at, tile_rows(tile), :] = value

        for number, group in enumerate(groups):
            group_pass(
                group, device_bits, tiles // chunks, rates,
                load if number else first_load, store, first_tile=chunk * (tiles // chunks),
            )

    def low_mix(slabs, vector):
        high, low = halves(jnp.concatenate(slabs, axis=0))
        right = lane_high[vector]
        values = dot(high, right) + (dot(low, right) + dot(high, lane_low[vector]))
        values = jnp.concatenate(
            [values[at * rows : (at + 1) * rows] for at in range(len(slabs))], axis=1
        )
        high, low = halves(values)
        left = mid_high[vector]
        values = dot(left, high) + (dot(left, low) + dot(mid_low[vector], high))
        return [values[:, at * LANES : (at + 1) * LANES] for at in range(len(slabs))]

    def turn_over(vector, held):
        rates = rates_of(rate_ref, vector, profile, local_bits, device_bits)
        groups = groups_of(device_bits)

        def load(at, tile):
            return held[at, tile_rows(tile), :]

        def store(at, tile, value):
            held[at, tile_rows(tile), :] = value

        def scale(at, tile):
            return scale_moved[at, tile_rows(tile), :]

        for group in groups[:-1]:
            group_pass(group, device_bits, tiles, rates, load, store)
        group_pass(groups[-1], device_bits, tiles, rates, load, store, scale)
        for group in groups[:-1]:
            group_pass(group, device_bits, tiles, rates, load, store)

    for chunk in range(chunks):
        loads[chunk].wait()
        prepare(0, send_a, chunk)
    pl.semaphore_wait(barrier, count - 1)

    def start_first(near, far, own):
        for turn in sent(near, far, own):
            copy(0, turn).start()

    each_pair(start_first)
    build_matrices()
    for chunk in range(chunks):
        prepare(1, send_b, chunk)

    def first_arrivals(near, far, own):
        turns = sent(near, far, own)
        for turn in turns:
            copy(0, turn).wait_send()
            copy(1, turn).start()
        for turn in turns:
            copy(0, turn).wait_recv()
        slabs = [near[1], far[1]]
        sources = [send_a if own else land_a, land_a]
        mixed = low_mix([source[flat, :rows, :] for source, flat in zip(sources, slabs)], 0)
        spread = expand([source[flat, rows:, :] for source, flat in zip(sources, slabs)])
        for at, flat in enumerate(slabs):
            land_a[flat, :rows, :] = mixed[at]
            scale_moved[flat] = spread[at * rows : (at + 1) * rows]

    each_pair(first_arrivals)
    turn_over(0, land_a)

    own_copy = pltpu.make_async_copy(back.at[1, me], out_ref.at[1, me], own_sem.at[0])

    def send_back(vector, landed, near, far, own):
        slabs = [near[1], far[1]]
        mixed = low_mix([landed[flat, :rows, :] for flat in slabs], vector)
        if own and vector == 0:
            land_c[me] = mixed[0]
        else:
            back[vector, slabs[0]] = mixed[0]
        back[vector, slabs[1]] = mixed[1]
        if own and vector == 1:
            own_copy.start()
        for turn in sent(near, far, own):
            copy(1 + vector, turn).wait_send()
            copy(2 + vector, turn).start()

    def second_arrivals(near, far, own):
        send_back(0, land_a, near, far, own)
        for turn in sent(near, far, own):
            copy(1, turn).wait_recv()
        slabs = [near[1], far[1]]
        sources = [send_b if own else land_b, land_b]
        mixed = low_mix([source[flat] for source, flat in zip(sources, slabs)], 1)
        for flat, values in zip(slabs, mixed):
            land_b[flat] = values

    each_pair(second_arrivals)
    turn_over(1, land_b)

    def third_arrivals(near, far, own):
        send_back(1, land_b, near, far, own)

    each_pair(third_arrivals)
    def third_landed(near, far, own):
        for turn in sent(near, far, own):
            copy(2, turn).wait_recv()

    each_pair(third_landed)
    rates = rates_of(rate_ref, 0, profile, low_bits, device_bits)
    for group in groups_of(device_bits):
        group_pass(
            group, device_bits, tiles, rates,
            lambda at, tile: land_c[at, tile_rows(tile), :],
            lambda at, tile, value: land_c.__setitem__((at, tile_rows(tile), slice(None)), value),
        )
    first_out = pltpu.make_async_copy(land_c, out_ref.at[0], own_sem.at[1])
    first_out.start()
    own_copy.wait()

    def last_arrivals(near, far, own):
        for turn in sent(near, far, own):
            copy(3, turn).wait()

    each_pair(last_arrivals)
    first_out.wait()


def finish_kernel(sizes, profile, land_ref, rate_ref, out_ref, held):
    device_bits, low_bits = sizes
    tiles = land_ref.shape[2] // ROWS
    groups = groups_of(device_bits)

    def tile_rows(tile):
        return pl.ds(pl.multiple_of(tile * ROWS, ROWS), ROWS)

    def landed(vector):
        return lambda at, tile: land_ref[vector, at, tile_rows(tile), :]

    def final(vector):
        def store(at, tile, value):
            out_ref[at, pl.ds(2 * ROWS * tile + vector, ROWS, stride=2), :] = value

        return store

    def load(at, tile):
        return held[at, tile_rows(tile), :]

    def store(at, tile, value):
        held[at, tile_rows(tile), :] = value

    group_pass(groups[0], device_bits, tiles, [], landed(0), final(0))
    rates = rates_of(rate_ref, 1, profile, low_bits, device_bits)
    for number, group in enumerate(groups):
        group_pass(
            group, device_bits, tiles, rates,
            load if number else landed(1),
            final(1) if number == len(groups) - 1 else store,
        )


def per_device(krylov, fitness_class, rate_index):
    vectors, length = krylov.shape
    wide, narrow = lax.axis_size("wide"), lax.axis_size("narrow")
    count = wide * narrow
    local_bits, device_bits = bits_of(length), bits_of(count)
    low_bits = local_bits - device_bits
    slab = length // count
    rows = slab // LANES
    per_row = LANES * fitness_class.shape[0] // length
    slab_classes = fitness_class.shape[0] // count
    interleaved = krylov.reshape(vectors, length // LANES, LANES).transpose(1, 0, 2)
    interleaved = interleaved.reshape(count, vectors * rows, LANES)
    classes = fitness_class.reshape(count, slab_classes)
    if slab_classes < LANES:
        classes = jnp.pad(classes, ((0, 0), (0, LANES - slab_classes)))
    classes = classes.reshape(count, -1, LANES)
    f32, bf16 = jnp.float32, jnp.bfloat16
    smem = pl.BlockSpec(memory_space=pltpu.SMEM)
    landed = pl.pallas_call(
        functools.partial(exchange_kernel, (wide, narrow, rows, local_bits, per_row)),
        out_shape=jax.ShapeDtypeStruct((vectors, count, rows, LANES), f32),
        in_specs=[pl.BlockSpec(memory_space=pl.ANY), pl.BlockSpec(memory_space=pl.ANY), smem],
        out_specs=pl.BlockSpec(memory_space=pl.ANY),
        scratch_shapes=[
            pltpu.VMEM((count, rows + classes.shape[1], LANES), f32),
            pltpu.VMEM((count, rows, LANES), f32),
            pltpu.VMEM((count, rows + classes.shape[1], LANES), f32),
            pltpu.VMEM((count, rows, LANES), f32),
            pltpu.VMEM((count, rows, LANES), f32),
            pltpu.VMEM((count, rows, LANES), f32),
            pltpu.VMEM((vectors, count, rows, LANES), f32),
            pltpu.VMEM((vectors, LANES, LANES), bf16),
            pltpu.VMEM((vectors, LANES, LANES), bf16),
            pltpu.VMEM((vectors, rows, rows), bf16),
            pltpu.VMEM((vectors, rows, rows), bf16),
            pltpu.VMEM((count, vectors * rows, LANES), f32),
            pltpu.VMEM(classes.shape, jnp.int32),
            pltpu.VMEM((count, rows, LANES), f32),
            pltpu.SemaphoreType.DMA((4, count)),
            pltpu.SemaphoreType.DMA((4, count)),
            pltpu.SemaphoreType.DMA((2,)),
            pltpu.SemaphoreType.DMA((5,)),
        ],
        compiler_params=pltpu.CompilerParams(
            collective_id=0, has_side_effects=True, vmem_limit_bytes=60 * 1024 * 1024
        ),
        name="exchange",
    )(interleaved, classes, rate_index)

    block = min(rows, 64)
    profile = profile_of(local_bits + device_bits)
    mixed = pl.pallas_call(
        functools.partial(finish_kernel, (device_bits, low_bits), profile),
        grid=(rows // block,),
        out_shape=jax.ShapeDtypeStruct((count, vectors * rows, LANES), f32),
        in_specs=[
            pl.BlockSpec((vectors, count, block, LANES), lambda step: (0, 0, step, 0)),
            smem,
        ],
        out_specs=pl.BlockSpec((count, vectors * block, LANES), lambda step: (0, step, 0)),
        scratch_shapes=[pltpu.VMEM((count, block, LANES), f32)],
        compiler_params=pltpu.CompilerParams(vmem_limit_bytes=60 * 1024 * 1024),
        name="finish",
    )(landed, rate_index)
    mixed = mixed.reshape(length // LANES, vectors, LANES).transpose(1, 0, 2)
    return mixed.reshape(vectors, length)


def solution(mesh):
    in_specs = (P(None, ("wide", "narrow")), P(("wide", "narrow")), P())
    out_specs = P(None, ("wide", "narrow"))
    return jax.shard_map(
        per_device, mesh=mesh, in_specs=in_specs, out_specs=out_specs, check_vma=False
    )
```

```python
import functools

import jax
import jax.numpy as jnp
import numpy as np
from jax import lax
from jax.experimental import pallas as pl
from jax.experimental.pallas import tpu as pltpu
from jax.sharding import PartitionSpec as P

LANES = 128
ROWS = 8
LANE_BITS = 7


def bits_of(count):
    return count.bit_length() - 1


def profile_of(total_bits):
    position = np.arange(total_bits, dtype=np.float32)
    return np.float32(1.0) + np.float32(0.5) * np.cos(np.float32(2.0) * position)


def rates_of(rate_ref, vector, profile, first, amount):
    level = 0.004 * (rate_ref[vector].astype(jnp.float32) + 1.0)
    return [level * float(profile[first + bit]) for bit in range(amount)]


def kron(rates, size):
    row = lax.broadcasted_iota(jnp.int32, (size, size), 0)
    column = lax.broadcasted_iota(jnp.int32, (size, size), 1)
    product = jnp.ones((size, size), jnp.float32)
    for bit, rate in enumerate(rates):
        agreeing = ((row >> bit) & 1) == ((column >> bit) & 1)
        product = product * jnp.where(agreeing, 1.0 - rate, rate)
    return product


def halves(values):
    high = values.astype(jnp.bfloat16)
    return high, (values - high.astype(jnp.float32)).astype(jnp.bfloat16)


def dot(left, right):
    return jnp.dot(left, right, preferred_element_type=jnp.float32)


def butterfly(values, rates):
    values = list(values)
    for bit, rate in enumerate(rates):
        step = 1 << bit
        for low in range(len(values)):
            if low & step:
                continue
            change = (values[low | step] - values[low]) * rate
            values[low] = values[low] + change
            values[low | step] = values[low | step] - change
    return values


def groups_of(bits):
    count = max(1, -(-bits // 5))
    groups, first = [], 0
    for number in range(count):
        amount = bits // count + (1 if number < bits % count else 0)
        groups.append((first, amount))
        first += amount
    return groups


def group_pass(group, bits, tiles, rates, load, store, scale=None, first_tile=0):
    first, amount = group
    low = 1 << first
    others = (1 << bits) // (1 << amount)
    part = rates[first : first + amount]

    def body(step, carry):
        tile = first_tile + step % tiles
        other = step // tiles
        base = (other // low) * (low << amount) + other % low
        index = [base + member * low for member in range(1 << amount)]
        values = butterfly([load(at, tile) for at in index], part)
        if scale is not None:
            values = [value * scale(at, tile) for value, at in zip(values, index)]
            values = butterfly(values, part)
        for at, value in zip(index, values):
            store(at, tile, value)
        return carry

    lax.fori_loop(0, others * tiles, body, 0)


def exchange_kernel(
    sizes, x_hbm, class_hbm, rate_ref, out_ref,
    send_a, send_b, land_a, land_b, scale_here, scale_moved, back, lane_high, lane_low,
    mid_high, mid_low, held, class_ref, land_c, send_sem, land_sem, own_sem, load_sem,
):
    wide, narrow, rows, local_bits, per_row = sizes
    count = wide * narrow
    wide_bits, narrow_bits = bits_of(wide), bits_of(narrow)
    device_bits = wide_bits + narrow_bits
    low_bits = local_bits - device_bits
    tiles = rows // ROWS
    class_rows = class_hbm.shape[1]
    profile = profile_of(local_bits + device_bits)
    my_wide, my_narrow = lax.axis_index("wide"), lax.axis_index("narrow")
    me = my_wide * narrow + my_narrow

    flips = [(1 << bit) * (1 - 2 * lax.rem(lax.div(me, 1 << bit), 2)) for bit in range(device_bits)]

    def partners(pair):
        near = me
        for bit in range(device_bits - 1):
            near = near + flips[bit] * lax.rem(lax.div(pair, 1 << bit), 2)
        return (pair, near), (pair + count // 2, near + flips[-1])

    def place(flat):
        return (lax.div(flat, narrow), lax.rem(flat, narrow))

    chunks = min(4, tiles)
    chunk_rows = 2 * rows // chunks
    class_load = pltpu.make_async_copy(class_hbm, class_ref, load_sem.at[chunks])
    class_load.start()
    loads = []
    for chunk in range(chunks):
        part = pl.ds(chunk * chunk_rows, chunk_rows)
        loads.append(
            pltpu.make_async_copy(x_hbm.at[:, part, :], held.at[:, part, :], load_sem.at[chunk])
        )
        loads[-1].start()

    barrier = pltpu.get_barrier_semaphore()

    def each_pair(step):
        step(*partners(0), True)

        def body(pair, carry):
            step(*partners(count // 2 - pair), False)
            return carry

        lax.fori_loop(1, count // 2, body, 0)

    def sent(near, far, own):
        return [far] if own else [far, near]

    def greet(near, far, own):
        for _, flat in sent(near, far, own):
            pl.semaphore_signal(
                barrier, inc=1, device_id=place(flat), device_id_type=pl.DeviceIdType.MESH
            )

    each_pair(greet)

    def copy(stage, turn):
        offset, flat = turn
        source, target = (
            (send_a, land_a), (send_b, land_b), (back.at[0], land_c), (back.at[1], out_ref.at[1])
        )[stage]
        return pltpu.make_async_remote_copy(
            src_ref=source.at[flat],
            dst_ref=target.at[me],
            send_sem=send_sem.at[stage, offset],
            recv_sem=land_sem.at[stage, offset],
            device_id=place(flat),
            device_id_type=pl.DeviceIdType.MESH,
        )

    def build_matrices():
        for vector in range(2):
            for high_ref, low_ref, first, size in (
                (lane_high, lane_low, 0, LANES),
                (mid_high, mid_low, LANE_BITS, rows),
            ):
                rates = rates_of(rate_ref, vector, profile, first, bits_of(size))
                high_ref[vector], low_ref[vector] = halves(kron(rates, size))

    def expand(compacts):
        span = min(rows, LANES // per_row)
        spread = jnp.concatenate(
            [
                jnp.broadcast_to(compact[at : at + 1], (span, LANES))
                for compact in compacts
                for at in range(class_rows)
            ],
            axis=0,
        )
        row = lax.broadcasted_iota(jnp.int32, spread.shape, 0)
        column = lax.broadcasted_iota(jnp.int32, spread.shape, 1)
        kept = jnp.where(row % span == column // per_row, spread, 0.0).astype(jnp.bfloat16)
        source = lax.broadcasted_iota(jnp.int32, (LANES, LANES), 0)
        lane = lax.broadcasted_iota(jnp.int32, (LANES, LANES), 1)
        pick = jnp.where(source % per_row == lane // (LANES // per_row), 1.0, 0.0)
        return dot(kept, pick.astype(jnp.bfloat16))

    together = min(8, count)

    def spread_here(step, carry):
        compacts = []
        for member in range(together):
            at = step * together + member
            compact = 0.5 + 0.25 * class_ref[at].astype(jnp.float32)
            send_a[at, rows:, :] = compact
            compacts.append(compact)
        spread = expand(compacts)
        for member in range(together):
            scale_here[step * together + member] = spread[member * rows : (member + 1) * rows]
        return carry

    class_load.wait()
    lax.fori_loop(0, count // together, spread_here, 0)

    def tile_rows(tile):
        return pl.ds(pl.multiple_of(tile * ROWS, ROWS), ROWS)

    def prepare(vector, target, chunk):
        rates = rates_of(rate_ref, vector, profile, low_bits, device_bits)
        groups = groups_of(device_bits)

        def first_load(at, tile):
            pairs = pl.ds(2 * ROWS * tile + vector, ROWS, stride=2)
            return held[at, pairs, :] * scale_here[at, tile_rows(tile), :]

        def load(at, tile):
            return target[at, tile_rows(tile), :]

        def store(at, tile, value):
            target[at, tile_rows(tile), :] = value

        for number, group in enumerate(groups):
            group_pass(
                group, device_bits, tiles // chunks, rates,
                load if number else first_load, store, first_tile=chunk * (tiles // chunks),
            )

    def low_mix(slabs, vector):
        high, low = halves(jnp.concatenate(slabs, axis=0))
        right = lane_high[vector]
        values = dot(high, right) + (dot(low, right) + dot(high, lane_low[vector]))
        values = jnp.concatenate(
            [values[at * rows : (at + 1) * rows] for at in range(len(slabs))], axis=1
        )
        high, low = halves(values)
        left = mid_high[vector]
        values = dot(left, high) + (dot(left, low) + dot(mid_low[vector], high))
        return [values[:, at * LANES : (at + 1) * LANES] for at in range(len(slabs))]

    def turn_over(vector, held):
        rates = rates_of(rate_ref, vector, profile, local_bits, device_bits)
        groups = groups_of(device_bits)

        def load(at, tile):
            return held[at, tile_rows(tile), :]

        def store(at, tile, value):
            held[at, tile_rows(tile), :] = value

        def scale(at, tile):
            return scale_moved[at, tile_rows(tile), :]

        for group in groups[:-1]:
            group_pass(group, device_bits, tiles, rates, load, store)
        group_pass(groups[-1], device_bits, tiles, rates, load, store, scale)
        for group in groups[:-1]:
            group_pass(group, device_bits, tiles, rates, load, store)

    for chunk in range(chunks):
        loads[chunk].wait()
        prepare(0, send_a, chunk)
    pl.semaphore_wait(barrier, count - 1)

    def start_first(near, far, own):
        for turn in sent(near, far, own):
            copy(0, turn).start()

    each_pair(start_first)
    build_matrices()
    for chunk in range(chunks):
        prepare(1, send_b, chunk)

    def first_arrivals(near, far, own):
        turns = sent(near, far, own)
        for turn in turns:
            copy(0, turn).wait_send()
            copy(1, turn).start()
        for turn in turns:
            copy(0, turn).wait_recv()
        slabs = [near[1], far[1]]
        sources = [send_a if own else land_a, land_a]
        mixed = low_mix([source[flat, :rows, :] for source, flat in zip(sources, slabs)], 0)
        spread = expand([source[flat, rows:, :] for source, flat in zip(sources, slabs)])
        for at, flat in enumerate(slabs):
            land_a[flat, :rows, :] = mixed[at]
            scale_moved[flat] = spread[at * rows : (at + 1) * rows]

    each_pair(first_arrivals)
    turn_over(0, land_a)

    own_copy = pltpu.make_async_copy(back.at[1, me], out_ref.at[1, me], own_sem.at[0])

    def send_back(vector, landed, near, far, own):
        slabs = [near[1], far[1]]
        mixed = low_mix([landed[flat, :rows, :] for flat in slabs], vector)
        if own and vector == 0:
            land_c[me] = mixed[0]
        else:
            back[vector, slabs[0]] = mixed[0]
        back[vector, slabs[1]] = mixed[1]
        if own and vector == 1:
            own_copy.start()
        for turn in sent(near, far, own):
            copy(1 + vector, turn).wait_send()
            copy(2 + vector, turn).start()

    def second_arrivals(near, far, own):
        send_back(0, land_a, near, far, own)
        for turn in sent(near, far, own):
            copy(1, turn).wait_recv()
        slabs = [near[1], far[1]]
        sources = [send_b if own else land_b, land_b]
        mixed = low_mix([source[flat] for source, flat in zip(sources, slabs)], 1)
        for flat, values in zip(slabs, mixed):
            land_b[flat] = values

    each_pair(second_arrivals)
    turn_over(1, land_b)

    def third_arrivals(near, far, own):
        send_back(1, land_b, near, far, own)

    each_pair(third_arrivals)
    def third_landed(near, far, own):
        for turn in sent(near, far, own):
            copy(2, turn).wait_recv()

    each_pair(third_landed)
    rates = rates_of(rate_ref, 0, profile, low_bits, device_bits)
    for group in groups_of(device_bits):
        group_pass(
            group, device_bits, tiles, rates,
            lambda at, tile: land_c[at, tile_rows(tile), :],
            lambda at, tile, value: land_c.__setitem__((at, tile_rows(tile), slice(None)), value),
        )
    first_out = pltpu.make_async_copy(land_c, out_ref.at[0], own_sem.at[1])
    first_out.start()
    own_copy.wait()

    def last_arrivals(near, far, own):
        for turn in sent(near, far, own):
            copy(3, turn).wait()

    each_pair(last_arrivals)
    first_out.wait()


def finish_kernel(sizes, profile, land_ref, rate_ref, out_ref, held):
    device_bits, low_bits = sizes
    tiles = land_ref.shape[2] // ROWS
    groups = groups_of(device_bits)

    def tile_rows(tile):
        return pl.ds(pl.multiple_of(tile * ROWS, ROWS), ROWS)

    def landed(vector):
        return lambda at, tile: land_ref[vector, at, tile_rows(tile), :]

    def final(vector):
        def store(at, tile, value):
            out_ref[at, pl.ds(2 * ROWS * tile + vector, ROWS, stride=2), :] = value

        return store

    def load(at, tile):
        return held[at, tile_rows(tile), :]

    def store(at, tile, value):
        held[at, tile_rows(tile), :] = value

    group_pass(groups[0], device_bits, tiles, [], landed(0), final(0))
    rates = rates_of(rate_ref, 1, profile, low_bits, device_bits)
    for number, group in enumerate(groups):
        group_pass(
            group, device_bits, tiles, rates,
            load if number else landed(1),
            final(1) if number == len(groups) - 1 else store,
        )


def per_device(krylov, fitness_class, rate_index):
    vectors, length = krylov.shape
    wide, narrow = lax.axis_size("wide"), lax.axis_size("narrow")
    count = wide * narrow
    local_bits, device_bits = bits_of(length), bits_of(count)
    low_bits = local_bits - device_bits
    slab = length // count
    rows = slab // LANES
    per_row = LANES * fitness_class.shape[0] // length
    slab_classes = fitness_class.shape[0] // count
    interleaved = krylov.reshape(vectors, length // LANES, LANES).transpose(1, 0, 2)
    interleaved = interleaved.reshape(count, vectors * rows, LANES)
    classes = fitness_class.reshape(count, slab_classes)
    if slab_classes < LANES:
        classes = jnp.pad(classes, ((0, 0), (0, LANES - slab_classes)))
    classes = classes.reshape(count, -1, LANES)
    f32, bf16 = jnp.float32, jnp.bfloat16
    smem = pl.BlockSpec(memory_space=pltpu.SMEM)
    landed = pl.pallas_call(
        functools.partial(exchange_kernel, (wide, narrow, rows, local_bits, per_row)),
        out_shape=jax.ShapeDtypeStruct((vectors, count, rows, LANES), f32),
        in_specs=[pl.BlockSpec(memory_space=pl.ANY), pl.BlockSpec(memory_space=pl.ANY), smem],
        out_specs=pl.BlockSpec(memory_space=pl.ANY),
        scratch_shapes=[
            pltpu.VMEM((count, rows + classes.shape[1], LANES), f32),
            pltpu.VMEM((count, rows, LANES), f32),
            pltpu.VMEM((count, rows + classes.shape[1], LANES), f32),
            pltpu.VMEM((count, rows, LANES), f32),
            pltpu.VMEM((count, rows, LANES), f32),
            pltpu.VMEM((count, rows, LANES), f32),
            pltpu.VMEM((vectors, count, rows, LANES), f32),
            pltpu.VMEM((vectors, LANES, LANES), bf16),
            pltpu.VMEM((vectors, LANES, LANES), bf16),
            pltpu.VMEM((vectors, rows, rows), bf16),
            pltpu.VMEM((vectors, rows, rows), bf16),
            pltpu.VMEM((count, vectors * rows, LANES), f32),
            pltpu.VMEM(classes.shape, jnp.int32),
            pltpu.VMEM((count, rows, LANES), f32),
            pltpu.SemaphoreType.DMA((4, count)),
            pltpu.SemaphoreType.DMA((4, count)),
            pltpu.SemaphoreType.DMA((2,)),
            pltpu.SemaphoreType.DMA((5,)),
        ],
        compiler_params=pltpu.CompilerParams(
            collective_id=0, has_side_effects=True, vmem_limit_bytes=60 * 1024 * 1024
        ),
        name="exchange",
    )(interleaved, classes, rate_index)

    block = min(rows, 64)
    profile = profile_of(local_bits + device_bits)
    mixed = pl.pallas_call(
        functools.partial(finish_kernel, (device_bits, low_bits), profile),
        grid=(rows // block,),
        out_shape=jax.ShapeDtypeStruct((count, vectors * rows, LANES), f32),
        in_specs=[
            pl.BlockSpec((vectors, count, block, LANES), lambda step: (0, 0, step, 0)),
            smem,
        ],
        out_specs=pl.BlockSpec((count, vectors * block, LANES), lambda step: (0, step, 0)),
        scratch_shapes=[pltpu.VMEM((count, block, LANES), f32)],
        compiler_params=pltpu.CompilerParams(vmem_limit_bytes=60 * 1024 * 1024),
        name="finish",
    )(landed, rate_index)
    mixed = mixed.reshape(length // LANES, vectors, LANES).transpose(1, 0, 2)
    return mixed.reshape(vectors, length)


def solution(mesh):
    in_specs = (P(None, ("wide", "narrow")), P(("wide", "narrow")), P())
    out_specs = P(None, ("wide", "narrow"))
    return jax.shard_map(
        per_device, mesh=mesh, in_specs=in_specs, out_specs=out_specs, check_vma=False
    )
```
